32 devices in a mesh: row: 4 (over y, core), col: 8 (over z, x).
Axes of the slice: x: 2, y: 2, z: 4, core: 2. Of those that a mesh axis runs over, the one named last changes fastest.
Arguments:
- start_block: bfloat16 [4096, 128], P(('row', 'col')), may hold values from -6 to 6
- matrix_tiles: bfloat16 [4, 4, 8, 2, 128, 128], P('row', None, 'col')
- tile_columns: int32 [4, 4, 8, 2], P('row', None, 'col'), may hold values from 0 to 7
- history: bfloat16 [4096, 512], P(('row', 'col'))
Outputs:
- new_block: float32 [4096, 128], P(('row', 'col'))
- coeffs: float32 [512, 128], replicated
The draws below stay inside these ranges and needn't reach their ends.
All inputs are finite; a program needn't handle non-finite values.
Results may differ from the reference program's by a relative error of at most 0.0029.
Values may be sent and summed in bfloat16 or wider, within the bound.
No kernel may reach another device: no remote copies, remote signals or barrier semaphores. Data moves between devices by JAX's collectives and lax.ppermute only.
A program may use at most 64 MiB of HBM per device.

```python
import jax
import jax.numpy as jnp
from jax import lax

TILE = 128
K = 128
SLOTS = 2
M = 512
NS = 4096
N_ROW = 4
N_COL = 8


def draw_matrix_tiles(key, part):
    full_shape = (N_ROW, N_ROW, N_COL, SLOTS, TILE, TILE)
    position = (jnp.arange(N_ROW)[:, None] * N_COL + jnp.arange(N_COL)[None, :]).astype(jnp.float32)
    fraction = position / (N_ROW * N_COL - 1)
    values = jnp.clip(jax.random.normal(key, full_shape, jnp.float32), -6.0, 6.0)
    spread = jnp.exp(jnp.log(0.3) + jnp.log(10.0) * fraction)
    factor = spread[None, :, :, None, None, None] / jnp.sqrt(jnp.float32(N_ROW * SLOTS * TILE))
    return (values * factor).astype(jnp.bfloat16)


def draw_history(key, part):
    noise_key = jax.random.fold_in(key, 11)
    shared_key = jax.random.fold_in(key, 12)
    loading_key = jax.random.fold_in(key, 13)
    noise = jnp.clip(jax.random.normal(noise_key, (NS, M), jnp.float32), -6.0, 6.0)
    shared = jnp.clip(jax.random.normal(shared_key, (NS,), jnp.float32), -6.0, 6.0)
    loading = jnp.clip(jax.random.normal(loading_key, (M,), jnp.float32), -6.0, 6.0)
    share = 0.15
    strength = jnp.sqrt(jnp.sqrt(jnp.float32(share * NS)) / jnp.float32(M))
    mixed = noise + strength * shared[:, None] * loading[None, :]
    return (mixed / jnp.sqrt(jnp.float32(NS))).astype(jnp.bfloat16)


def place_ends(array, rng, least, largest):
    longest = array.shape.index(max(array.shape))
    spots = []
    for shift in (0, 1):
        where = [jax.random.randint(jax.random.fold_in(rng, axis), (), 0, length) for axis, length in enumerate(array.shape)]
        where[longest] = (where[longest] + shift) % array.shape[longest]
        spots.append(tuple(where))
    return array.at[spots[0]].set(least).at[spots[1]].set(largest)


def levels(rng, dims, pieces, smallest, top_value):
    level = 1.0
    for dim, blocks in pieces:
        heights = jax.random.uniform(jax.random.fold_in(jax.random.fold_in(rng, 6), dim), (blocks,), jnp.float32, smallest / len(pieces), top_value / len(pieces))
        level = level * jnp.repeat(jnp.exp(heights), dims[dim] // blocks).reshape((-1,) + (1,) * (len(dims) - 1 - dim))
    return level


def scatter_about(stream_key, shape, deviation, most, pieces=(), kind=jnp.bfloat16):
    array = jax.random.normal(stream_key, shape, jnp.float32) * deviation
    if len(pieces) > 0:
        array = levels(stream_key, shape, pieces, -0.22, 0.18) * array
    return jnp.clip(array, min=-most, max=most).astype(kind)


def setup_inputs(seed: int = 0) -> dict:
    seeds = jax.random.split(jax.random.key(seed), 5)
    start_block = scatter_about(seeds[0], (NS, K), 1.0, 6.0, ((0, 32),))
    matrix_tiles = draw_matrix_tiles(jax.random.fold_in(seeds[4], 71), 0)
    tile_columns = place_ends(jax.random.randint(seeds[2], (N_ROW, N_ROW, N_COL, SLOTS), 0, N_COL), jax.random.fold_in(seeds[2], 1), 0, N_COL - 1).astype(jnp.int32)
    history = draw_history(jax.random.fold_in(seeds[4], 71), 0)
    return dict(start_block=start_block, matrix_tiles=matrix_tiles, tile_columns=tile_columns, history=history)


def apply_matrix(vectors, matrix_tiles, tile_columns):

    def add_block(running, block_index):
        vector_block = lax.dynamic_slice_in_dim(vectors, block_index * (N_COL * TILE), N_COL * TILE, 0).reshape(N_COL, TILE, K)
        column_ids = lax.dynamic_index_in_dim(tile_columns, block_index, 0, keepdims=False)
        picked = vector_block[column_ids]
        tiles_here = lax.dynamic_index_in_dim(matrix_tiles, block_index, 0, keepdims=False)
        product = jnp.einsum('rcsij,rcsjk->rcik', tiles_here.astype(jnp.float32), picked.astype(jnp.float32))
        return (running + product, None)
    starting = jnp.zeros((N_ROW, N_COL, TILE, K), jnp.float32)
    summed, unused = lax.scan(add_block, starting, jnp.arange(N_ROW, dtype=jnp.int32))
    return summed.reshape(N_ROW * N_COL * TILE, K)

def reference(start_block, matrix_tiles, tile_columns, history):
    first_power = apply_matrix(start_block, matrix_tiles, tile_columns).astype(jnp.bfloat16)
    second_power = apply_matrix(first_power, matrix_tiles, tile_columns)
    filtered = 2.0 * second_power - start_block.astype(jnp.float32)
    history_wide = history.astype(jnp.float32)
    coeffs = jnp.dot(history_wide.T, filtered, precision=lax.Precision.HIGHEST)
    cleaned = filtered - jnp.dot(history_wide, coeffs, precision=lax.Precision.HIGHEST)
    lengths = jnp.sqrt(lax.optimization_barrier(jnp.mean(cleaned * cleaned, axis=0)) + 1e-05)
    return (cleaned / lengths[None, :], coeffs)
```

```python
import functools

import jax
import jax.numpy as jnp
from jax import lax
from jax.experimental import pallas as pl
from jax.experimental.pallas import tpu as pltpu
from jax.sharding import PartitionSpec as P

F32 = jnp.float32
BF16 = jnp.bfloat16
PAD = 16
VMEM = pl.BlockSpec(memory_space=pltpu.VMEM)
SMEM = pl.BlockSpec(memory_space=pltpu.SMEM)


def nbytes(tree):
    return sum(a.size * a.dtype.itemsize for a in jax.tree.leaves(tree))


def call(kernel, out, args, n_smem, out_specs=None):
    single = jax.tree.structure(out) == jax.tree.structure(0)
    if out_specs is None:
        out_specs = VMEM if single else jax.tree.map(lambda _: VMEM, out)
    room = 2 * (nbytes(args) + nbytes(out)) + 8 * 2**20
    return pl.pallas_call(
        kernel,
        out_shape=out,
        in_specs=[SMEM] * n_smem + [VMEM] * (len(args) - n_smem),
        out_specs=out_specs,
        compiler_params=pltpu.CompilerParams(vmem_limit_bytes=min(room, 56 * 2**20)),
    )(*args)


def nt(a, b):
    return lax.dot_general(a, b, (((1,), (1,)), ((), ())), preferred_element_type=F32)


def pieces(value):
    high = value.astype(BF16)
    rest = value - high.astype(F32)
    middle = rest.astype(BF16)
    low = (rest - middle.astype(F32)).astype(BF16)
    return jnp.concatenate([high, middle, low], axis=0)


def joined(stacked):
    third = stacked.shape[0] // 3
    return (stacked[2 * third :] + stacked[third : 2 * third]) + stacked[:third]


def prepare(columns_ref, start_ref, tiles_ref, parts_ref, packed_ref):
    n_row, n_col, width, _ = parts_ref.shape
    turned = start_ref[...].astype(F32).T
    for r in range(n_row):
        part = turned[r * width : (r + 1) * width].astype(BF16)
        for c in range(n_col):
            parts_ref[r, c] = part
    rows = tiles_ref.shape[0]
    packed_ref[:rows] = tiles_ref[...]
    lane = lax.broadcasted_iota(jnp.int32, (PAD, packed_ref.shape[1]), 1)
    numbers = jnp.zeros(lane.shape, jnp.int32)
    for i in range(columns_ref.shape[0]):
        numbers = jnp.where(lane == i, columns_ref[i], numbers)
    packed_ref[rows:] = numbers.astype(F32).astype(BF16)


def multiply(me_row, n_row, slots, order, columns, segment, tiles, p):
    total = None
    for q in range(n_row):
        block = me_row ^ q
        for s in range(slots):
            picked = segment(block, columns(q, p * slots + s))
            start = (p * slots + s) * order
            if not isinstance(start, int):
                start = pl.multiple_of(start, order)
            term = nt(picked, tiles[q][pl.ds(start, order), :])
            total = term if total is None else total + term
    return total


def each(count, body):
    if count <= 4:
        for i in range(count):
            body(i)
    else:
        pl.loop(0, count)(body)


def first(n_row, groups, slots, me_ref, parts_ref, *refs):
    tiles, (copies_ref, columns_ref) = refs[:n_row], refs[n_row:]
    order = parts_ref.shape[-1]
    rows = groups * slots * order
    lane = lax.broadcasted_iota(jnp.int32, (PAD, order), 1)
    for q in range(n_row):
        numbers = tiles[q][rows:, :].astype(F32).astype(jnp.int32)
        for i in range(groups * slots):
            columns_ref[q, i] = jnp.max(jnp.where(lane == i, numbers, 0))

    def row(p):
        total = multiply(
            me_ref[0], n_row, slots, order, lambda q, i: columns_ref[q, i],
            lambda b, c: parts_ref[b, c], tiles, p,
        )
        value = total.astype(BF16)
        for c in range(copies_ref.shape[0]):
            copies_ref[c, p] = value

    each(groups, row)


def second(n_row, groups, slots, me_ref, columns_ref, parts_ref, vectors_ref, *refs):
    tiles, history, (filtered_ref, coeffs_ref) = refs[:n_row], refs[n_row : 2 * n_row], refs[2 * n_row :]
    order = parts_ref.shape[-1]

    def row(p):
        total = multiply(
            me_ref[0], n_row, slots, order, lambda q, i: columns_ref[q, i],
            lambda b, c: vectors_ref[c, b], tiles, p,
        )
        filtered_ref[p] = 2.0 * total - parts_ref[p, me_ref[1]].astype(F32)

    each(groups, row)
    total = None
    for q in range(n_row):
        split = pieces(filtered_ref[me_ref[0] ^ q])
        term = joined(jnp.dot(split, history[q][...], preferred_element_type=F32))
        total = term if total is None else total + term
    coeffs_ref[...] = total


def clean(n_row, me_ref, coeffs_ref, filtered_ref, *refs):
    history, outs, squares_ref = refs[:n_row], refs[n_row : 2 * n_row], refs[2 * n_row]
    width, order = filtered_ref.shape[1:]
    stored = coeffs_ref.shape[1]
    coeffs = coeffs_ref[...]
    split = pieces(coeffs)
    squares = jnp.zeros((width, order), F32)
    for q in range(n_row):
        cleaned = filtered_ref[me_ref[0] ^ q] - joined(nt(split, history[q][...]))
        squares = squares + cleaned * cleaned
        outs[q][:, :stored] = coeffs
        outs[q][:, stored:] = cleaned
    sums = jnp.sum(squares.T, axis=0, keepdims=True)
    line = jnp.concatenate([sums] * n_row, axis=1)
    lane = lax.broadcasted_iota(jnp.int32, line.shape, 1)
    mine = (lane >= me_ref[0] * width) & (lane < (me_ref[0] + 1) * width)
    line = jnp.where(mine, line, 0.0)
    squares_ref[...] = jnp.broadcast_to(line[:, None, :], squares_ref.shape)


def finish(n_row, total_rows, me_ref, squares_ref, *refs):
    slabs, (block_ref, out_ref, whole_ref) = refs[:n_row], refs[n_row:]
    width = slabs[0].shape[0]
    stored = out_ref.shape[0]
    for q in range(n_row):
        r = me_ref[0] ^ q
        whole_ref[pl.ds(pl.multiple_of(r * width, width), width), :] = slabs[q][...]
    sums = jnp.sum(squares_ref[...], axis=0)[:1]
    lengths = jnp.sqrt(sums / total_rows + 1e-05)
    out_ref[...] = whole_ref[:, :stored].T
    block_ref[...] = whole_ref[:, stored:].T / lengths


def exchanged(value, axis, q):
    return lax.ppermute(value, axis, [(i, i ^ q) for i in range(lax.axis_size(axis))])


def per_device(start_block, matrix_tiles, tile_columns, history):
    n_row, n_col = lax.axis_size("row"), lax.axis_size("col")
    me_row, me_col = lax.axis_index("row"), lax.axis_index("col")
    me = jnp.stack([me_row, me_col]).astype(jnp.int32)
    _, groups, _, slots, order, _ = matrix_tiles.shape
    n_vectors = start_block.shape[1]
    stored = history.shape[1]
    width = n_vectors // n_row
    rows = groups * slots * order
    both = ("row", "col")

    parts, packed = call(
        prepare,
        (
            jax.ShapeDtypeStruct((n_row, n_col, width, order), BF16),
            jax.ShapeDtypeStruct((rows + PAD, order), BF16),
        ),
        (tile_columns.reshape(-1), start_block, matrix_tiles.reshape(rows, order)),
        1,
    )
    tiles = [packed] + [exchanged(packed, "row", q) for q in range(1, n_row)]
    parts = lax.all_to_all(
        parts.reshape(n_row * n_col, width, order), both, 0, 0
    ).reshape(n_row, n_col, width, order)
    histories = [history] + [exchanged(history, "row", q) for q in range(1, n_row)]

    copies, columns = call(
        functools.partial(first, n_row, groups, slots),
        (
            jax.ShapeDtypeStruct((n_col, groups, width, order), BF16),
            jax.ShapeDtypeStruct((n_row, groups * slots), jnp.int32),
        ),
        (me, parts, *tiles),
        1,
        (VMEM, SMEM),
    )
    vectors = lax.all_to_all(copies, "col", 0, 0)
    filtered, coeffs = call(
        functools.partial(second, n_row, groups, slots),
        (
            jax.ShapeDtypeStruct((groups, width, order), F32),
            jax.ShapeDtypeStruct((width, stored), F32),
        ),
        (me, columns, parts, vectors, *tiles, *histories),
        2,
    )
    step = 1
    while step < n_col:
        coeffs = coeffs + exchanged(coeffs, "col", step)
        step *= 2
    *slabs, squares = call(
        functools.partial(clean, n_row),
        [jax.ShapeDtypeStruct((width, stored + order), F32) for _ in range(n_row)]
        + [jax.ShapeDtypeStruct((n_row * n_col, 1, n_vectors), F32)],
        (me, coeffs, filtered, *histories),
        1,
    )
    slabs = [slabs[0]] + [exchanged(slabs[q], "row", q) for q in range(1, n_row)]
    squares = lax.all_to_all(squares, both, 0, 0)
    total_rows = order * n_row * n_col
    out = (
        jax.ShapeDtypeStruct((order, n_vectors), F32),
        jax.ShapeDtypeStruct((stored, n_vectors), F32),
    )
    args = (me, squares, *slabs)
    return pl.pallas_call(
        functools.partial(finish, n_row, total_rows),
        out_shape=out,
        in_specs=[SMEM] + [VMEM] * (len(args) - 1),
        out_specs=(VMEM, VMEM),
        scratch_shapes=[pltpu.VMEM((n_vectors, stored + order), F32)],
        compiler_params=pltpu.CompilerParams(vmem_limit_bytes=2 * nbytes(args) + 16 * 2**20),
    )(*args)


def solution(mesh):
    in_specs = (
        P(("row", "col"), None),
        P("row", None, "col", None, None, None),
        P("row", None, "col", None),
        P(("row", "col"), None),
    )
    out_specs = (P(("row", "col"), None), P())
    return jax.shard_map(
        per_device, mesh=mesh, in_specs=in_specs, out_specs=out_specs, check_vma=False
    )
```

```python
import functools

import jax
import jax.numpy as jnp
from jax import lax
from jax.experimental import pallas as pl
from jax.experimental.pallas import tpu as pltpu
from jax.sharding import PartitionSpec as P

F32 = jnp.float32
BF16 = jnp.bfloat16
VMEM = pl.BlockSpec(memory_space=pltpu.VMEM)
SMEM = pl.BlockSpec(memory_space=pltpu.SMEM)


def nbytes(tree):
    return sum(a.size * a.dtype.itemsize for a in jax.tree.leaves(tree))


def call(kernel, out, args, n_smem, out_specs=None):
    single = jax.tree.structure(out) == jax.tree.structure(0)
    if out_specs is None:
        out_specs = VMEM if single else jax.tree.map(lambda _: VMEM, out)
    room = 2 * (nbytes(args) + nbytes(out)) + 8 * 2**20
    return pl.pallas_call(
        kernel,
        out_shape=out,
        in_specs=[SMEM] * n_smem + [VMEM] * (len(args) - n_smem),
        out_specs=out_specs,
        compiler_params=pltpu.CompilerParams(vmem_limit_bytes=min(room, 56 * 2**20)),
    )(*args)


def nt(a, b):
    return lax.dot_general(a, b, (((1,), (1,)), ((), ())), preferred_element_type=F32)


def pieces(value):
    high = value.astype(BF16)
    rest = value - high.astype(F32)
    middle = rest.astype(BF16)
    low = (rest - middle.astype(F32)).astype(BF16)
    return jnp.concatenate([high, middle, low], axis=0)


def joined(stacked):
    third = stacked.shape[0] // 3
    return (stacked[2 * third :] + stacked[third : 2 * third]) + stacked[:third]


def prepare(start_ref, parts_ref):
    n_row, n_col, width, _ = parts_ref.shape
    turned = start_ref[...].astype(F32).T
    for r in range(n_row):
        part = turned[r * width : (r + 1) * width].astype(BF16)
        for c in range(n_col):
            parts_ref[r, c] = part


def multiply(me_row, n_row, slots, order, columns, segment, tiles, p):
    total = None
    for q in range(n_row):
        block = me_row ^ q
        for s in range(slots):
            picked = segment(block, columns(q, p * slots + s))
            start = (p * slots + s) * order
            if not isinstance(start, int):
                start = pl.multiple_of(start, order)
            term = nt(picked, tiles[q][pl.ds(start, order), :])
            total = term if total is None else total + term
    return total


def each(count, body):
    if count <= 4:
        for i in range(count):
            body(i)
    else:
        pl.loop(0, count)(body)


def first(n_row, groups, slots, me_ref, columns_ref, parts_ref, *refs):
    tiles, copies_ref = refs[:n_row], refs[n_row]
    order = parts_ref.shape[-1]

    def row(p):
        total = multiply(
            me_ref[0], n_row, slots, order, lambda q, i: columns_ref[q, i],
            lambda b, c: parts_ref[b, c], tiles, p,
        )
        value = total.astype(BF16)
        for c in range(copies_ref.shape[0]):
            copies_ref[c, p] = value

    each(groups, row)


def second(n_row, groups, slots, me_ref, columns_ref, parts_ref, vectors_ref, *refs):
    tiles, history, (filtered_ref, coeffs_ref) = refs[:n_row], refs[n_row : 2 * n_row], refs[2 * n_row :]
    order = parts_ref.shape[-1]

    def row(p):
        total = multiply(
            me_ref[0], n_row, slots, order, lambda q, i: columns_ref[q, i],
            lambda b, c: vectors_ref[c, b], tiles, p,
        )
        filtered_ref[p] = 2.0 * total - parts_ref[p, me_ref[1]].astype(F32)

    each(groups, row)
    total = None
    for q in range(n_row):
        split = pieces(filtered_ref[me_ref[0] ^ q])
        term = joined(jnp.dot(split, history[q][...], preferred_element_type=F32))
        total = term if total is None else total + term
    coeffs_ref[...] = total


def clean(n_row, me_ref, coeffs_ref, filtered_ref, *refs):
    history, outs, squares_ref = refs[:n_row], refs[n_row : 2 * n_row], refs[2 * n_row]
    width, order = filtered_ref.shape[1:]
    stored = coeffs_ref.shape[1]
    coeffs = coeffs_ref[...]
    split = pieces(coeffs)
    squares = jnp.zeros((width, order), F32)
    for q in range(n_row):
        cleaned = filtered_ref[me_ref[0] ^ q] - joined(nt(split, history[q][...]))
        squares = squares + cleaned * cleaned
        outs[q][:, :stored] = coeffs
        outs[q][:, stored:] = cleaned
    sums = jnp.sum(squares.T, axis=0, keepdims=True)
    line = jnp.concatenate([sums] * n_row, axis=1)
    lane = lax.broadcasted_iota(jnp.int32, line.shape, 1)
    mine = (lane >= me_ref[0] * width) & (lane < (me_ref[0] + 1) * width)
    line = jnp.where(mine, line, 0.0)
    squares_ref[...] = jnp.broadcast_to(line[:, None, :], squares_ref.shape)


def finish(n_row, total_rows, me_ref, squares_ref, *refs):
    slabs, (block_ref, out_ref, whole_ref) = refs[:n_row], refs[n_row:]
    width = slabs[0].shape[0]
    stored = out_ref.shape[0]
    for q in range(n_row):
        r = me_ref[0] ^ q
        whole_ref[pl.ds(pl.multiple_of(r * width, width), width), :] = slabs[q][...]
    sums = jnp.sum(squares_ref[...], axis=0)[:1]
    lengths = jnp.sqrt(sums / total_rows + 1e-05)
    out_ref[...] = whole_ref[:, :stored].T
    block_ref[...] = whole_ref[:, stored:].T / lengths


def from_rows(value):
    n_row = lax.axis_size("row")
    found = {0: value}
    bit = n_row // 2
    while bit:
        found |= {q | bit: exchanged(found[q], "row", bit) for q in list(found)}
        bit //= 2
    return [found[q] for q in range(n_row)]


def exchanged(value, axis, q):
    return lax.ppermute(value, axis, [(i, i ^ q) for i in range(lax.axis_size(axis))])


def per_device(start_block, matrix_tiles, tile_columns, history):
    n_row, n_col = lax.axis_size("row"), lax.axis_size("col")
    me_row, me_col = lax.axis_index("row"), lax.axis_index("col")
    me = jnp.stack([me_row, me_col]).astype(jnp.int32)
    _, groups, _, slots, order, _ = matrix_tiles.shape
    n_vectors = start_block.shape[1]
    stored = history.shape[1]
    width = n_vectors // n_row
    rows = groups * slots * order
    both = ("row", "col")

    tiles = from_rows(matrix_tiles.reshape(rows, order))
    parts = call(
        prepare, jax.ShapeDtypeStruct((n_row, n_col, width, order), BF16), (start_block,), 0
    )
    parts = lax.all_to_all(
        parts.reshape(n_row * n_col, width, order), both, 0, 0
    ).reshape(n_row, n_col, width, order)
    histories = from_rows(history)
    columns = jnp.stack(from_rows(tile_columns.reshape(-1)))

    copies = call(
        functools.partial(first, n_row, groups, slots),
        jax.ShapeDtypeStruct((n_col, groups, width, order), BF16),
        (me, columns, parts, *tiles),
        2,
    )
    vectors = lax.all_to_all(copies, "col", 0, 0)
    filtered, coeffs = call(
        functools.partial(second, n_row, groups, slots),
        (
            jax.ShapeDtypeStruct((groups, width, order), F32),
            jax.ShapeDtypeStruct((width, stored), F32),
        ),
        (me, columns, parts, vectors, *tiles, *histories),
        2,
    )
    step = 1
    while step < n_col:
        coeffs = coeffs + exchanged(coeffs, "col", step)
        step *= 2
    *slabs, squares = call(
        functools.partial(clean, n_row),
        [jax.ShapeDtypeStruct((width, stored + order), F32) for _ in range(n_row)]
        + [jax.ShapeDtypeStruct((n_row * n_col, 1, n_vectors), F32)],
        (me, coeffs, filtered, *histories),
        1,
    )
    slabs = [slabs[0]] + [exchanged(slabs[q], "row", q) for q in range(1, n_row)]
    squares = lax.all_to_all(squares, both, 0, 0)
    total_rows = order * n_row * n_col
    out = (
        jax.ShapeDtypeStruct((order, n_vectors), F32),
        jax.ShapeDtypeStruct((stored, n_vectors), F32),
    )
    args = (me, squares, *slabs)
    return pl.pallas_call(
        functools.partial(finish, n_row, total_rows),
        out_shape=out,
        in_specs=[SMEM] + [VMEM] * (len(args) - 1),
        out_specs=(VMEM, VMEM),
        scratch_shapes=[pltpu.VMEM((n_vectors, stored + order), F32)],
        compiler_params=pltpu.CompilerParams(vmem_limit_bytes=2 * nbytes(args) + 16 * 2**20),
    )(*args)


def solution(mesh):
    in_specs = (
        P(("row", "col"), None),
        P("row", None, "col", None, None, None),
        P("row", None, "col", None),
        P(("row", "col"), None),
    )
    out_specs = (P(("row", "col"), None), P())
    return jax.shard_map(
        per_device, mesh=mesh, in_specs=in_specs, out_specs=out_specs, check_vma=False
    )
```

```python
import functools

import jax
import jax.numpy as jnp
from jax import lax
from jax.experimental import pallas as pl
from jax.experimental.pallas import tpu as pltpu
from jax.sharding import PartitionSpec as P

F32 = jnp.float32
BF16 = jnp.bfloat16
PAD = 16
LINES = 8
VMEM = pl.BlockSpec(memory_space=pltpu.VMEM)
BOTH = ("row", "col")


def nbytes(tree):
    return sum(a.size * a.dtype.itemsize for a in jax.tree.leaves(tree))


def call(kernel, out, args, scratch=()):
    held = [jax.ShapeDtypeStruct(shape, kind) for shape, kind in scratch]
    room = 2 * (nbytes(args) + nbytes(out) + nbytes(held)) + 8 * 2**20
    return pl.pallas_call(
        kernel,
        out_shape=out,
        in_specs=[VMEM] * len(args),
        out_specs=jax.tree.map(lambda _: VMEM, out),
        scratch_shapes=[pltpu.VMEM(shape, kind) for shape, kind in scratch],
        compiler_params=pltpu.CompilerParams(vmem_limit_bytes=min(room, 56 * 2**20)),
    )(*args)


def position(lanes):
    row, col = lax.axis_index("row"), lax.axis_index("col")
    return row >> 1, row & 1, col >> (lanes - 1), col & (lanes - 1)


def place(entry, core):
    (even_q, even_u), (odd_q, odd_u) = entry
    return jnp.where(core == 0, even_q, odd_q), jnp.where(core == 0, even_u, odd_u)


def nt(a, b):
    return lax.dot_general(a, b, (((1,), (1,)), ((), ())), preferred_element_type=F32)


def pieces(value):
    high = value.astype(BF16)
    rest = value - high.astype(F32)
    middle = rest.astype(BF16)
    low = (rest - middle.astype(F32)).astype(BF16)
    return jnp.concatenate([high, middle, low], axis=0)


def joined(stacked):
    third = stacked.shape[0] // 3
    return (stacked[2 * third :] + stacked[third : 2 * third]) + stacked[:third]


def each(count, body):
    if count <= 4:
        for i in range(count):
            body(i)
    else:
        pl.loop(0, count)(body)


def prepare(lanes, width, columns_ref, start_ref, parts_ref):
    n_block, n_col, rows, order = parts_ref.shape
    groups, slots = columns_ref.shape
    lane = lax.broadcasted_iota(jnp.int32, (PAD, order), 1)
    numbers = jnp.zeros(lane.shape, jnp.int32)
    for p in range(groups):
        for s in range(slots):
            numbers = jnp.where(lane == p * slots + s, columns_ref[p, s], numbers)
    numbers = numbers.astype(F32).astype(BF16)
    turned = start_ref[...].astype(F32).T
    for r in range(n_block):
        for u in range(lanes):
            first_row = (r * lanes + u) * width
            part = turned[first_row : first_row + width].astype(BF16)
            for c in range(u, n_col, lanes):
                parts_ref[r, c, :width] = part
                parts_ref[r, c, rows - PAD :] = numbers


def multiply(near, lanes, slots, columns_ref, segment, tiles, sums_ref):
    groups, order = sums_ref.shape[1], sums_ref.shape[3]
    block, core, _, _ = position(lanes)
    for i, tile_ref in tiles:
        q, u = place(near[i], core)

        def row(p):
            total = None
            for s in range(slots):
                start = (p * slots + s) * order
                if not isinstance(start, int):
                    start = pl.multiple_of(start, order)
                picked = segment(block ^ q, columns_ref[i, p * slots + s, 0])
                term = nt(picked, tile_ref[pl.ds(start, order), :])
                total = term if total is None else total + term
            sums_ref[u, p] += total

        each(groups, row)


def first(near, early, lanes, slots, parts_ref, *refs):
    tiles, (sums_ref, columns_ref, start_ref) = refs[:early], refs[early:]
    _, groups, width, order = sums_ref.shape
    block, core, me_z, me_lane = position(lanes)
    rows = parts_ref.shape[2]
    for i, entry in enumerate(near):
        q, u = place(entry, core)
        numbers = parts_ref[block ^ q, me_z * lanes + (me_lane ^ u), rows - PAD :]
        columns_ref[i] = numbers.astype(F32)[:LINES].T.astype(jnp.int32)
    for u in range(lanes):
        for r in range(parts_ref.shape[0]):
            start_ref[u, r] = parts_ref[r, me_z * lanes + (me_lane ^ u), :width]
    sums_ref[...] = jnp.zeros_like(sums_ref)
    multiply(
        near, lanes, slots, columns_ref, lambda b, c: parts_ref[b, c, :width],
        list(enumerate(tiles)), sums_ref,
    )


def rest(near, early, slots, columns_ref, parts_ref, before_ref, *refs):
    tiles, (keep_ref, give_ref, sums_ref) = refs[: len(near) - early], refs[len(near) - early :]
    lanes, n_block, width, _ = keep_ref.shape
    _, core, _, _ = position(lanes)
    sums_ref[...] = before_ref[...]
    multiply(
        near, lanes, slots, columns_ref, lambda b, c: parts_ref[b, c, :width],
        list(enumerate(tiles, early)), sums_ref,
    )
    for u in range(lanes):
        for r in range(n_block):
            keep_ref[u, r] = sums_ref[u, 2 * r + core]
            give_ref[u, r] = sums_ref[u, 2 * r + (1 - core)]


def second(near, slots, n_vectors, columns_ref, start_ref, *refs):
    count = len(near)
    vectors, tiles, refs = refs[:n_vectors], refs[n_vectors : n_vectors + count], refs[n_vectors + count :]
    keep_ref, give_ref, sums_ref = refs[:3]
    lanes, n_block, _, _ = keep_ref.shape
    _, core, me_z, me_lane = position(lanes)
    if n_vectors > 1:
        all_ref = refs[3]
        for k in range(n_vectors):
            all_ref[me_z ^ k] = vectors[k][...]
    else:
        all_ref = vectors[0]

    def segment(b, c):
        return all_ref[c >> (lanes - 1), (c & (lanes - 1)) ^ me_lane, b]

    sums_ref[...] = jnp.zeros_like(sums_ref)
    multiply(near, lanes, slots, columns_ref, segment, list(enumerate(tiles)), sums_ref)
    for u in range(lanes):
        for r in range(n_block):
            keep_ref[u, r] = 2.0 * sums_ref[u, 2 * r + core] - start_ref[u, r].astype(F32)
            give_ref[u, r] = 2.0 * sums_ref[u, 2 * r + (1 - core)]


def project(near, keep_ref, given_ref, *refs):
    history, (filtered_ref, coeffs_keep_ref, coeffs_give_ref) = refs[: len(near)], refs[len(near) :]
    lanes = keep_ref.shape[0]
    block, core, _, _ = position(lanes)
    filtered_ref[...] = keep_ref[...] + given_ref[...]
    total = None
    for i, entry in enumerate(near):
        q, u = place(entry, core)
        split = pieces(filtered_ref[u, block ^ q])
        term = joined(jnp.dot(split, history[i][...], preferred_element_type=F32))
        total = term if total is None else total + term
    half = total.shape[1] // 2
    low, high = total[:, :half], total[:, half:]
    coeffs_keep_ref[...] = jnp.where(core == 0, low, high)
    coeffs_give_ref[...] = jnp.where(core == 0, high, low)


def clean(near, mine_ref, mate_ref, filtered_ref, *refs):
    count = len(near)
    history, outs, squares_ref = refs[:count], refs[count : 2 * count], refs[2 * count]
    lanes, _, width, order = filtered_ref.shape
    block, core, _, me_lane = position(lanes)
    mine, mate = mine_ref[...], mate_ref[...]
    coeffs = jnp.concatenate(
        [jnp.where(core == 0, mine, mate), jnp.where(core == 0, mate, mine)], axis=1
    )
    stored = coeffs.shape[1]
    split = pieces(coeffs)
    squares = jnp.zeros((width, order), F32)
    for i, entry in enumerate(near):
        q, u = place(entry, core)
        cleaned = filtered_ref[u, block ^ q] - joined(nt(split, history[i][...]))
        squares = squares + cleaned * cleaned
        outs[i][:, :stored] = coeffs
        outs[i][:, stored:] = cleaned
    sums = jnp.sum(squares.T, axis=0, keepdims=True)
    n_vectors = squares_ref.shape[2]
    line = jnp.concatenate([sums] * (n_vectors // width), axis=1)
    lane = lax.broadcasted_iota(jnp.int32, line.shape, 1)
    begin = (block * lanes + me_lane) * width
    line = jnp.where((lane >= begin) & (lane < begin + width), line, 0.0)
    squares_ref[...] = jnp.broadcast_to(line[:, None, :], squares_ref.shape)


def finish(near, lanes, total_rows, squares_ref, *refs):
    slabs, (block_ref, out_ref, whole_ref) = refs[:-3], refs[-3:]
    width = slabs[0].shape[0]
    stored = out_ref.shape[0]
    block, core, _, me_lane = position(lanes)
    for slab, entry in zip(slabs, near):
        q, u = place(entry, core)
        start = ((block ^ q) * lanes + (me_lane ^ u)) * width
        whole_ref[pl.ds(pl.multiple_of(start, width), width), :] = slab[...]
    sums = jnp.sum(squares_ref[...], axis=0)[:1]
    lengths = jnp.sqrt(sums / total_rows + 1e-05)
    out_ref[...] = whole_ref[:, :stored].T
    block_ref[...] = whole_ref[:, stored:].T / lengths


def neighbours(n_block, lanes):
    found = [((0, 0), (0, 0))]
    bit = n_block // 2
    if lanes == 2:
        found.append(((0, 1), (bit, 0)) if bit else ((0, 1), (0, 1)))
    if lanes == 2 and bit:
        found += [((bit, 0), (0, 1)), ((bit, 1), (bit, 1))]
        bit //= 2
    while bit:
        found += [((a ^ bit, u), (b ^ bit, v)) for (a, u), (b, v) in found]
        bit //= 2
    return found


def crossed(value, entry):
    n_row, n_col = lax.axis_size("row"), lax.axis_size("col")
    pairs = []
    for r in range(n_row):
        q, u = entry[r % 2]
        pairs += [(r * n_col + c, (r ^ (2 * q)) * n_col + (c ^ u)) for c in range(n_col)]
    return lax.ppermute(value, BOTH, pairs)


def spread(found, near):
    while len(found) < len(near):
        found = found + [crossed(a, near[len(found)]) for a in found]
    return found


def swapped(value, q, u):
    n_row, n_col = lax.axis_size("row"), lax.axis_size("col")
    pairs = [(r * n_col + c, (r ^ q) * n_col + (c ^ u)) for r in range(n_row) for c in range(n_col)]
    return lax.ppermute(value, BOTH, pairs)


def per_device(start_block, matrix_tiles, tile_columns, history):
    n_row, n_col = lax.axis_size("row"), lax.axis_size("col")
    _, groups, _, slots, order, _ = matrix_tiles.shape
    n_vectors = start_block.shape[1]
    stored = history.shape[1]
    rows = groups * slots * order
    n_block = n_row // 2
    lanes = 2 if n_col % 2 == 0 else 1
    width = n_vectors // (n_block * lanes)
    members = n_col // lanes
    few = members <= 4
    near = neighbours(n_block, lanes)
    count = len(near)
    early = count - count // 4

    def over_members(value):
        return [value] + [swapped(value, 0, k * lanes) for k in range(1, members)]

    def mate(value):
        return swapped(value, 1, 0)

    plane = lanes == 2 and n_block > 1
    tiles = [matrix_tiles.reshape(rows, order)]
    if plane:
        tiles += lax.optimization_barrier([crossed(tiles[0], entry) for entry in near[1:3]])
        tiles.append(crossed(tiles[1], near[2]))
    tiles = spread(tiles, near)
    tall = -(-width // PAD) * PAD + PAD
    parts = call(
        functools.partial(prepare, lanes, width),
        jax.ShapeDtypeStruct((n_block, n_col, tall, order), BF16),
        (tile_columns.reshape(groups, slots), start_block),
    )
    cores = [
        [(2 * r + core) * n_col + c for r in range(n_block) for c in range(n_col)] for core in range(2)
    ]
    parts = lax.all_to_all(
        parts.reshape(n_block * n_col, tall, order), BOTH, 0, 0, axis_index_groups=cores
    ).reshape(n_block, n_col, tall, order)
    own = [history]
    if plane:
        history, tiles[2] = lax.optimization_barrier((history, tiles[2]))
        own += [crossed(history, entry) for entry in near[1:3]]

    piece = (lanes, n_block, width, order)
    sums = ((lanes, groups, width, order), F32)
    before, columns, start = call(
        functools.partial(first, near, early, lanes, slots),
        [
            jax.ShapeDtypeStruct(sums[0], F32),
            jax.ShapeDtypeStruct((count, order, LINES), jnp.int32),
            jax.ShapeDtypeStruct(piece, BF16),
        ],
        (parts, *tiles[:early]),
    )
    if plane:
        tiles[early], *own = lax.optimization_barrier((tiles[early], *own))
    keep, give = call(
        functools.partial(rest, near, early, slots),
        [jax.ShapeDtypeStruct(piece, F32)] * 2,
        (columns, parts, before, *tiles[early:]),
        [sums],
    )
    if plane:
        keep, own[1] = lax.optimization_barrier((keep, own[1]))
        own.append(crossed(own[1], near[2]))
    own = spread(own, near)
    mine = (keep + mate(give)).astype(BF16)
    if few:
        vectors = over_members(mine)
    else:
        alike = [list(range(u, n_col, lanes)) for u in range(lanes)]
        vectors = [
            lax.all_to_all(
                jnp.broadcast_to(mine, (members,) + piece), "col", 0, 0, axis_index_groups=alike
            )
        ]
    keep, give = call(
        functools.partial(second, near, slots, len(vectors)),
        [jax.ShapeDtypeStruct(piece, F32)] * 2,
        (columns, start, *vectors, *tiles),
        [sums] + ([((members,) + piece, BF16)] if few else []),
    )
    filtered, coeffs, coeffs_give = call(
        functools.partial(project, near),
        [jax.ShapeDtypeStruct(piece, F32)] + [jax.ShapeDtypeStruct((width, stored // 2), F32)] * 2,
        (keep, mate(give), *own),
    )
    coeffs = coeffs + mate(coeffs_give)
    if members == 4:
        zero, one, two, three = over_members(coeffs)
        coeffs = (zero + one) + (two + three)
    else:
        step = lanes
        while step < n_col:
            coeffs = coeffs + swapped(coeffs, 0, step)
            step *= 2
    slab = jax.ShapeDtypeStruct((width, stored + order), F32)
    copies = 1
    while nbytes(slab) > n_row * n_col * copies * n_vectors * 4:
        copies *= 2
    *slabs, squares = call(
        functools.partial(clean, near),
        [slab] * count + [jax.ShapeDtypeStruct((n_row * n_col, copies, n_vectors), F32)],
        (coeffs, mate(coeffs), filtered, *own),
    )
    slabs = [slabs[0]] + [crossed(a, entry) for a, entry in zip(slabs[1:], near[1:])]
    squares = lax.all_to_all(squares, BOTH, 0, 0)
    return call(
        functools.partial(finish, near, lanes, order * n_row * n_col),
        (
            jax.ShapeDtypeStruct((order, n_vectors), F32),
            jax.ShapeDtypeStruct((stored, n_vectors), F32),
        ),
        (squares, *slabs),
        [((n_vectors, stored + order), F32)],
    )


def solution(mesh):
    in_specs = (
        P(("row", "col"), None),
        P("row", None, "col", None, None, None),
        P("row", None, "col", None),
        P(("row", "col"), None),
    )
    out_specs = (P(("row", "col"), None), P())
    return jax.shard_map(
        per_device, mesh=mesh, in_specs=in_specs, out_specs=out_specs, check_vma=False
    )
```

```python
import functools

import jax
import jax.numpy as jnp
from jax import lax
from jax.experimental import pallas as pl
from jax.experimental.pallas import tpu as pltpu
from jax.sharding import PartitionSpec as P

F32 = jnp.float32
BF16 = jnp.bfloat16
PAD = 16
LINES = 8
VMEM = pl.BlockSpec(memory_space=pltpu.VMEM)
BOTH = ("row", "col")


def nbytes(tree):
    return sum(a.size * a.dtype.itemsize for a in jax.tree.leaves(tree))


def call(kernel, out, args, scratch=()):
    held = [jax.ShapeDtypeStruct(shape, kind) for shape, kind in scratch]
    room = 2 * (nbytes(args) + nbytes(out) + nbytes(held)) + 8 * 2**20
    return pl.pallas_call(
        kernel,
        out_shape=out,
        in_specs=[VMEM] * len(args),
        out_specs=jax.tree.map(lambda _: VMEM, out),
        scratch_shapes=[pltpu.VMEM(shape, kind) for shape, kind in scratch],
        compiler_params=pltpu.CompilerParams(vmem_limit_bytes=min(room, 56 * 2**20)),
    )(*args)


def position(lanes):
    row, col = lax.axis_index("row"), lax.axis_index("col")
    return row >> 1, row & 1, col >> (lanes - 1), col & (lanes - 1)


def place(entry, core):
    (even_q, even_u), (odd_q, odd_u) = entry
    return jnp.where(core == 0, even_q, odd_q), jnp.where(core == 0, even_u, odd_u)


def nt(a, b):
    return lax.dot_general(a, b, (((1,), (1,)), ((), ())), preferred_element_type=F32)


def pieces(value):
    high = value.astype(BF16)
    rest = value - high.astype(F32)
    middle = rest.astype(BF16)
    low = (rest - middle.astype(F32)).astype(BF16)
    return jnp.concatenate([high, middle, low], axis=0)


def joined(stacked):
    third = stacked.shape[0] // 3
    return (stacked[2 * third :] + stacked[third : 2 * third]) + stacked[:third]


def each(count, body):
    if count <= 4:
        for i in range(count):
            body(i)
    else:
        pl.loop(0, count)(body)


def prepare(lanes, width, columns_ref, start_ref, parts_ref):
    n_block, n_col, rows, order = parts_ref.shape
    groups, slots = columns_ref.shape
    lane = lax.broadcasted_iota(jnp.int32, (PAD, order), 1)
    numbers = jnp.zeros(lane.shape, jnp.int32)
    for p in range(groups):
        for s in range(slots):
            numbers = jnp.where(lane == p * slots + s, columns_ref[p, s], numbers)
    numbers = numbers.astype(F32).astype(BF16)
    turned = start_ref[...].astype(F32).T
    for r in range(n_block):
        for u in range(lanes):
            first_row = (r * lanes + u) * width
            part = turned[first_row : first_row + width].astype(BF16)
            for c in range(u, n_col, lanes):
                parts_ref[r, c, :width] = part
                parts_ref[r, c, rows - PAD :] = numbers


def multiply(near, lanes, slots, columns_ref, segment, tiles, sums_ref):
    groups, order = sums_ref.shape[1], sums_ref.shape[3]
    block, core, _, _ = position(lanes)
    for i, tile_ref in tiles:
        q, u = place(near[i], core)

        def row(p):
            total = None
            for s in range(slots):
                start = (p * slots + s) * order
                if not isinstance(start, int):
                    start = pl.multiple_of(start, order)
                picked = segment(block ^ q, columns_ref[i, p * slots + s, 0])
                term = nt(picked, tile_ref[pl.ds(start, order), :])
                total = term if total is None else total + term
            sums_ref[u, p] += total

        each(groups, row)


def first(near, early, lanes, slots, parts_ref, *refs):
    tiles, (sums_ref, columns_ref, start_ref) = refs[:early], refs[early:]
    _, groups, width, order = sums_ref.shape
    block, core, me_z, me_lane = position(lanes)
    rows = parts_ref.shape[2]
    for i, entry in enumerate(near):
        q, u = place(entry, core)
        numbers = parts_ref[block ^ q, me_z * lanes + (me_lane ^ u), rows - PAD :]
        columns_ref[i] = numbers.astype(F32)[:LINES].T.astype(jnp.int32)
    for u in range(lanes):
        for r in range(parts_ref.shape[0]):
            start_ref[u, r] = parts_ref[r, me_z * lanes + (me_lane ^ u), :width]
    sums_ref[...] = jnp.zeros_like(sums_ref)
    multiply(
        near, lanes, slots, columns_ref, lambda b, c: parts_ref[b, c, :width],
        list(enumerate(tiles)), sums_ref,
    )


def rest(near, early, slots, columns_ref, parts_ref, before_ref, *refs):
    tiles, (keep_ref, give_ref, sums_ref) = refs[: len(near) - early], refs[len(near) - early :]
    lanes, n_block, width, _ = keep_ref.shape
    _, core, _, _ = position(lanes)
    sums_ref[...] = before_ref[...]
    multiply(
        near, lanes, slots, columns_ref, lambda b, c: parts_ref[b, c, :width],
        list(enumerate(tiles, early)), sums_ref,
    )
    for u in range(lanes):
        for r in range(n_block):
            keep_ref[u, r] = sums_ref[u, 2 * r + core]
            give_ref[u, r] = sums_ref[u, 2 * r + (1 - core)]


def second(near, slots, n_vectors, columns_ref, start_ref, *refs):
    count = len(near)
    vectors, tiles, refs = refs[:n_vectors], refs[n_vectors : n_vectors + count], refs[n_vectors + count :]
    keep_ref, give_ref, sums_ref = refs[:3]
    lanes, n_block, _, _ = keep_ref.shape
    _, core, me_z, me_lane = position(lanes)
    if n_vectors > 1:
        all_ref = refs[3]
        for k in range(n_vectors):
            all_ref[me_z ^ k] = vectors[k][...]
    else:
        all_ref = vectors[0]

    def segment(b, c):
        return all_ref[c >> (lanes - 1), (c & (lanes - 1)) ^ me_lane, b]

    sums_ref[...] = jnp.zeros_like(sums_ref)
    multiply(near, lanes, slots, columns_ref, segment, list(enumerate(tiles)), sums_ref)
    for u in range(lanes):
        for r in range(n_block):
            keep_ref[u, r] = 2.0 * sums_ref[u, 2 * r + core] - start_ref[u, r].astype(F32)
            give_ref[u, r] = 2.0 * sums_ref[u, 2 * r + (1 - core)]


def project(near, keep_ref, given_ref, *refs):
    history, (filtered_ref, coeffs_keep_ref, coeffs_give_ref) = refs[: len(near)], refs[len(near) :]
    lanes = keep_ref.shape[0]
    block, core, _, _ = position(lanes)
    filtered_ref[...] = keep_ref[...] + given_ref[...]
    total = None
    for i, entry in enumerate(near):
        q, u = place(entry, core)
        split = pieces(filtered_ref[u, block ^ q])
        term = joined(jnp.dot(split, history[i][...], preferred_element_type=F32))
        total = term if total is None else total + term
    half = total.shape[1] // 2
    low, high = total[:, :half], total[:, half:]
    coeffs_keep_ref[...] = jnp.where(core == 0, low, high)
    coeffs_give_ref[...] = jnp.where(core == 0, high, low)


def clean(near, mine_ref, mate_ref, filtered_ref, *refs):
    count = len(near)
    history, outs, squares_ref = refs[:count], refs[count : 2 * count], refs[2 * count]
    lanes, _, width, order = filtered_ref.shape
    block, core, _, me_lane = position(lanes)
    mine, mate = mine_ref[...], mate_ref[...]
    coeffs = jnp.concatenate(
        [jnp.where(core == 0, mine, mate), jnp.where(core == 0, mate, mine)], axis=1
    )
    stored = coeffs.shape[1]
    split = pieces(coeffs)
    squares = jnp.zeros((width, order), F32)
    for i, entry in enumerate(near):
        q, u = place(entry, core)
        cleaned = filtered_ref[u, block ^ q] - joined(nt(split, history[i][...]))
        squares = squares + cleaned * cleaned
        outs[i][:, :stored] = coeffs
        outs[i][:, stored:] = cleaned
    sums = jnp.sum(squares.T, axis=0, keepdims=True)
    n_vectors = squares_ref.shape[2]
    line = jnp.concatenate([sums] * (n_vectors // width), axis=1)
    lane = lax.broadcasted_iota(jnp.int32, line.shape, 1)
    begin = (block * lanes + me_lane) * width
    line = jnp.where((lane >= begin) & (lane < begin + width), line, 0.0)
    squares_ref[...] = jnp.broadcast_to(line[:, None, :], squares_ref.shape)


def finish(near, lanes, total_rows, squares_ref, *refs):
    slabs, (block_ref, out_ref, whole_ref) = refs[:-3], refs[-3:]
    width = slabs[0].shape[0]
    stored = out_ref.shape[0]
    block, core, _, me_lane = position(lanes)
    for slab, entry in zip(slabs, near[::-1]):
        q, u = place(entry, core)
        start = ((block ^ q) * lanes + (me_lane ^ u)) * width
        whole_ref[pl.ds(pl.multiple_of(start, width), width), :] = slab[...]
    sums = jnp.sum(squares_ref[...], axis=0)[:1]
    lengths = jnp.sqrt(sums / total_rows + 1e-05)
    out_ref[...] = whole_ref[:, :stored].T
    block_ref[...] = whole_ref[:, stored:].T / lengths


def neighbours(n_block, lanes):
    found = [((0, 0), (0, 0))]
    bit = n_block // 2
    if lanes == 2:
        found.append(((0, 1), (bit, 0)) if bit else ((0, 1), (0, 1)))
    if lanes == 2 and bit:
        found += [((bit, 0), (0, 1)), ((bit, 1), (bit, 1))]
        bit //= 2
    while bit:
        found += [((a ^ bit, u), (b ^ bit, v)) for (a, u), (b, v) in found]
        bit //= 2
    return found


def crossed(value, entry):
    n_row, n_col = lax.axis_size("row"), lax.axis_size("col")
    pairs = []
    for r in range(n_row):
        q, u = entry[r % 2]
        pairs += [(r * n_col + c, (r ^ (2 * q)) * n_col + (c ^ u)) for c in range(n_col)]
    return lax.ppermute(value, BOTH, pairs)


def spread(found, near):
    while len(found) < len(near):
        found = found + [crossed(a, near[len(found)]) for a in found]
    return found


def swapped(value, q, u):
    n_row, n_col = lax.axis_size("row"), lax.axis_size("col")
    pairs = [(r * n_col + c, (r ^ q) * n_col + (c ^ u)) for r in range(n_row) for c in range(n_col)]
    return lax.ppermute(value, BOTH, pairs)


def per_device(start_block, matrix_tiles, tile_columns, history):
    n_row, n_col = lax.axis_size("row"), lax.axis_size("col")
    _, groups, _, slots, order, _ = matrix_tiles.shape
    n_vectors = start_block.shape[1]
    stored = history.shape[1]
    rows = groups * slots * order
    n_block = n_row // 2
    lanes = 2 if n_col % 2 == 0 else 1
    width = n_vectors // (n_block * lanes)
    members = n_col // lanes
    few = members <= 4
    near = neighbours(n_block, lanes)
    count = len(near)
    early = count - count // 4

    def over_members(value):
        return [value] + [swapped(value, 0, k * lanes) for k in range(1, members)]

    def mate(value):
        return swapped(value, 1, 0)

    plane = lanes == 2 and n_block > 1
    tiles = [matrix_tiles.reshape(rows, order)]
    if plane:
        tiles += lax.optimization_barrier([crossed(tiles[0], entry) for entry in near[1:3]])
        tiles.append(crossed(tiles[1], near[2]))
    tiles = spread(tiles, near)
    tall = -(-width // PAD) * PAD + PAD
    parts = call(
        functools.partial(prepare, lanes, width),
        jax.ShapeDtypeStruct((n_block, n_col, tall, order), BF16),
        (tile_columns.reshape(groups, slots), start_block),
    )
    cores = [
        [(2 * r + core) * n_col + c for r in range(n_block) for c in range(n_col)] for core in range(2)
    ]
    parts = lax.all_to_all(
        parts.reshape(n_block * n_col, tall, order), BOTH, 0, 0, axis_index_groups=cores
    ).reshape(n_block, n_col, tall, order)
    own = [history]
    if plane:
        history, tiles[2] = lax.optimization_barrier((history, tiles[2]))
        own += [crossed(history, entry) for entry in near[1:3]]

    piece = (lanes, n_block, width, order)
    sums = ((lanes, groups, width, order), F32)
    before, columns, start = call(
        functools.partial(first, near, early, lanes, slots),
        [
            jax.ShapeDtypeStruct(sums[0], F32),
            jax.ShapeDtypeStruct((count, order, LINES), jnp.int32),
            jax.ShapeDtypeStruct(piece, BF16),
        ],
        (parts, *tiles[:early]),
    )
    keep, give = call(
        functools.partial(rest, near, early, slots),
        [jax.ShapeDtypeStruct(piece, F32)] * 2,
        (columns, parts, before, *tiles[early:]),
        [sums],
    )
    if plane:
        own.append(crossed(own[1], near[2]))
    own = spread(own, near)
    mine = (keep + mate(give)).astype(BF16)
    if few:
        vectors = over_members(mine)
    else:
        alike = [list(range(u, n_col, lanes)) for u in range(lanes)]
        vectors = [
            lax.all_to_all(
                jnp.broadcast_to(mine, (members,) + piece), "col", 0, 0, axis_index_groups=alike
            )
        ]
    keep, give = call(
        functools.partial(second, near, slots, len(vectors)),
        [jax.ShapeDtypeStruct(piece, F32)] * 2,
        (columns, start, *vectors, *tiles),
        [sums] + ([((members,) + piece, BF16)] if few else []),
    )
    filtered, coeffs, coeffs_give = call(
        functools.partial(project, near),
        [jax.ShapeDtypeStruct(piece, F32)] + [jax.ShapeDtypeStruct((width, stored // 2), F32)] * 2,
        (keep, mate(give), *own),
    )
    coeffs = coeffs + mate(coeffs_give)
    if members == 4:
        zero, one, two, three = over_members(coeffs)
        coeffs = (zero + one) + (two + three)
    else:
        step = lanes
        while step < n_col:
            coeffs = coeffs + swapped(coeffs, 0, step)
            step *= 2
    slab = jax.ShapeDtypeStruct((width, stored + order), F32)
    copies = 1
    while nbytes(slab) > 2 * n_row * n_col * copies * n_vectors * 4:
        copies *= 2
    *slabs, squares = call(
        functools.partial(clean, near),
        [slab] * count + [jax.ShapeDtypeStruct((n_row * n_col, copies, n_vectors), F32)],
        (coeffs, mate(coeffs), filtered, *own),
    )
    slabs = [slabs[0]] + [crossed(a, entry) for a, entry in zip(slabs[1:], near[1:])]
    squares = lax.all_to_all(squares, BOTH, 0, 0)
    return call(
        functools.partial(finish, near, lanes, order * n_row * n_col),
        (
            jax.ShapeDtypeStruct((order, n_vectors), F32),
            jax.ShapeDtypeStruct((stored, n_vectors), F32),
        ),
        (squares, *slabs[::-1]),
        [((n_vectors, stored + order), F32)],
    )


def solution(mesh):
    in_specs = (
        P(("row", "col"), None),
        P("row", None, "col", None, None, None),
        P("row", None, "col", None),
        P(("row", "col"), None),
    )
    out_specs = (P(("row", "col"), None), P())
    return jax.shard_map(
        per_device, mesh=mesh, in_specs=in_specs, out_specs=out_specs, check_vma=False
    )
```

```python
import functools

import jax
import jax.numpy as jnp
from jax import lax
from jax.experimental import pallas as pl
from jax.experimental.pallas import tpu as pltpu
from jax.sharding import PartitionSpec as P

F32 = jnp.float32
BF16 = jnp.bfloat16
PAD = 16
LINES = 8
VMEM = pl.BlockSpec(memory_space=pltpu.VMEM)
BOTH = ("row", "col")


def nbytes(tree):
    return sum(a.size * a.dtype.itemsize for a in jax.tree.leaves(tree))


def call(kernel, out, args, scratch=()):
    held = [jax.ShapeDtypeStruct(shape, kind) for shape, kind in scratch]
    room = 2 * (nbytes(args) + nbytes(out) + nbytes(held)) + 8 * 2**20
    return pl.pallas_call(
        kernel,
        out_shape=out,
        in_specs=[VMEM] * len(args),
        out_specs=jax.tree.map(lambda _: VMEM, out),
        scratch_shapes=[pltpu.VMEM(shape, kind) for shape, kind in scratch],
        compiler_params=pltpu.CompilerParams(vmem_limit_bytes=min(room, 56 * 2**20)),
    )(*args)


def position(lanes):
    row, col = lax.axis_index("row"), lax.axis_index("col")
    return row >> 1, row & 1, col >> (lanes - 1), col & (lanes - 1)


def place(entry, core):
    (even_q, even_u), (odd_q, odd_u) = entry
    return jnp.where(core == 0, even_q, odd_q), jnp.where(core == 0, even_u, odd_u)


def nt(a, b):
    return lax.dot_general(a, b, (((1,), (1,)), ((), ())), preferred_element_type=F32)


def pieces(value):
    high = value.astype(BF16)
    rest = value - high.astype(F32)
    middle = rest.astype(BF16)
    low = (rest - middle.astype(F32)).astype(BF16)
    return jnp.concatenate([high, middle, low], axis=0)


def joined(stacked):
    third = stacked.shape[0] // 3
    return (stacked[2 * third :] + stacked[third : 2 * third]) + stacked[:third]


def each(count, body):
    if count <= 4:
        for i in range(count):
            body(i)
    else:
        pl.loop(0, count)(body)


def prepare(lanes, width, columns_ref, start_ref, parts_ref):
    n_block, n_col, rows, order = parts_ref.shape
    slots, groups = columns_ref.shape
    lane = lax.broadcasted_iota(jnp.int32, (PAD, order), 1)
    numbers = jnp.zeros(lane.shape, jnp.int32)
    for p in range(groups):
        for s in range(slots):
            numbers = jnp.where(lane == p * slots + s, columns_ref[s, p], numbers)
    numbers = numbers.astype(F32).astype(BF16)
    turned = start_ref[...].astype(F32).T
    for r in range(n_block):
        for u in range(lanes):
            first_row = (r * lanes + u) * width
            part = turned[first_row : first_row + width].astype(BF16)
            for c in range(u, n_col, lanes):
                parts_ref[r, c, :width] = part
                parts_ref[r, c, rows - PAD :] = numbers


def multiply(near, lanes, slots, columns_ref, segment, tiles, sums_ref):
    groups, order = sums_ref.shape[1], sums_ref.shape[3]
    block, core, _, _ = position(lanes)
    for i, tile_ref in tiles:
        q, u = place(near[i], core)

        def row(p):
            total = None
            for s in range(slots):
                start = (p * slots + s) * order
                if not isinstance(start, int):
                    start = pl.multiple_of(start, order)
                picked = segment(block ^ q, columns_ref[i, p * slots + s, 0])
                term = nt(picked, tile_ref[pl.ds(start, order), :])
                total = term if total is None else total + term
            sums_ref[u, p] += total

        each(groups, row)


def first(near, early, lanes, slots, parts_ref, *refs):
    tiles, (sums_ref, columns_ref, start_ref) = refs[:early], refs[early:]
    _, groups, width, order = sums_ref.shape
    block, core, me_z, me_lane = position(lanes)
    rows = parts_ref.shape[2]
    for i, entry in enumerate(near):
        q, u = place(entry, core)
        numbers = parts_ref[block ^ q, me_z * lanes + (me_lane ^ u), rows - PAD :]
        columns_ref[i] = numbers.astype(F32)[:LINES].T.astype(jnp.int32)
    for u in range(lanes):
        for r in range(parts_ref.shape[0]):
            start_ref[u, r] = parts_ref[r, me_z * lanes + (me_lane ^ u), :width]
    sums_ref[...] = jnp.zeros_like(sums_ref)
    multiply(
        near, lanes, slots, columns_ref, lambda b, c: parts_ref[b, c, :width],
        list(enumerate(tiles)), sums_ref,
    )


def rest(near, early, slots, columns_ref, parts_ref, before_ref, *refs):
    tiles, (keep_ref, give_ref, sums_ref) = refs[: len(near) - early], refs[len(near) - early :]
    lanes, n_block, width, _ = keep_ref.shape
    _, core, _, _ = position(lanes)
    sums_ref[...] = before_ref[...]
    multiply(
        near, lanes, slots, columns_ref, lambda b, c: parts_ref[b, c, :width],
        list(enumerate(tiles, early)), sums_ref,
    )
    for u in range(lanes):
        for r in range(n_block):
            keep_ref[u, r] = sums_ref[u, 2 * r + core]
            give_ref[u, r] = sums_ref[u, 2 * r + (1 - core)]


def second(near, slots, n_vectors, columns_ref, start_ref, *refs):
    count = len(near)
    vectors, tiles, refs = refs[:n_vectors], refs[n_vectors : n_vectors + count], refs[n_vectors + count :]
    out_ref, sums_ref = refs[:2]
    lanes, n_block, _, _ = start_ref.shape
    _, core, me_z, me_lane = position(lanes)
    if n_vectors > 1:
        all_ref = refs[2]
        for k in range(n_vectors):
            all_ref[me_z ^ k] = vectors[k][...]
    else:
        all_ref = vectors[0]

    def segment(b, c):
        return all_ref[c >> (lanes - 1), (c & (lanes - 1)) ^ me_lane, b]

    sums_ref[...] = jnp.zeros_like(sums_ref)
    multiply(near, lanes, slots, columns_ref, segment, list(enumerate(tiles)), sums_ref)
    for u in range(lanes):
        for r in range(n_block):
            out_ref[u, 2 * r + core] = 2.0 * sums_ref[u, 2 * r + core] - start_ref[u, r].astype(F32)
            out_ref[u, 2 * r + (1 - core)] = 2.0 * sums_ref[u, 2 * r + (1 - core)]


def project(near, ours_ref, theirs_ref, *refs):
    history, (filtered_ref, coeffs_ref) = refs[: len(near)], refs[len(near) :]
    lanes = ours_ref.shape[0]
    block, core, _, _ = position(lanes)
    filtered_ref[...] = ours_ref[...] + theirs_ref[...]
    total = None
    for i, entry in enumerate(near):
        q, u = place(entry, core)
        for side in range(2):
            split = pieces(filtered_ref[u, 2 * (block ^ q) + side])
            term = joined(jnp.dot(split, history[i][side], preferred_element_type=F32))
            total = term if total is None else total + term
    coeffs_ref[...] = total


def correct(near, coeffs_ref, *refs):
    history, (keep_ref, give_ref) = refs[: len(near)], refs[len(near) :]
    lanes = keep_ref.shape[0]
    block, core, _, _ = position(lanes)
    split = pieces(coeffs_ref[...])
    for i, entry in enumerate(near):
        q, u = place(entry, core)
        keep_ref[u, block ^ q] = joined(nt(split, history[i][core]))
        give_ref[u, block ^ q] = joined(nt(split, history[i][1 - core]))


def clean(near, mine_ref, mate_ref, filtered_ref, ours_ref, theirs_ref, *refs):
    count = len(near)
    outs, squares_ref = refs[:count], refs[count]
    lanes, _, width, order = ours_ref.shape
    block, core, _, me_lane = position(lanes)
    mine, mate = mine_ref[...], mate_ref[...]
    coeffs = jnp.concatenate(
        [jnp.where(core == 0, mine, mate), jnp.where(core == 0, mate, mine)], axis=1
    )
    stored = coeffs.shape[1]
    squares = jnp.zeros((width, order), F32)
    for i, entry in enumerate(near):
        q, u = place(entry, core)
        r = block ^ q
        cleaned = filtered_ref[u, 2 * r + core] - (ours_ref[u, r] + theirs_ref[u, r])
        squares = squares + cleaned * cleaned
        outs[i][:, :stored] = coeffs
        outs[i][:, stored:] = cleaned
    sums = jnp.sum(squares.T, axis=0, keepdims=True)
    n_vectors = squares_ref.shape[2]
    line = jnp.concatenate([sums] * (n_vectors // width), axis=1)
    lane = lax.broadcasted_iota(jnp.int32, line.shape, 1)
    begin = (block * lanes + me_lane) * width
    line = jnp.where((lane >= begin) & (lane < begin + width), line, 0.0)
    squares_ref[...] = jnp.broadcast_to(line[:, None, :], squares_ref.shape)


def finish(near, lanes, total_rows, squares_ref, *refs):
    slabs, (block_ref, out_ref, whole_ref) = refs[:-3], refs[-3:]
    width = slabs[0].shape[0]
    stored = out_ref.shape[0]
    block, core, _, me_lane = position(lanes)
    for slab, entry in zip(slabs, near[::-1]):
        q, u = place(entry, core)
        start = ((block ^ q) * lanes + (me_lane ^ u)) * width
        whole_ref[pl.ds(pl.multiple_of(start, width), width), :] = slab[...]
    sums = jnp.sum(squares_ref[...], axis=0)[:1]
    lengths = jnp.sqrt(sums / total_rows + 1e-05)
    out_ref[...] = whole_ref[:, :stored].T
    block_ref[...] = whole_ref[:, stored:].T / lengths


def neighbours(n_block, lanes):
    found = [((0, 0), (0, 0))]
    bit = n_block // 2
    if lanes == 2:
        found.append(((0, 1), (bit, 0)) if bit else ((0, 1), (0, 1)))
    if lanes == 2 and bit:
        found += [((bit, 0), (0, 1)), ((bit, 1), (bit, 1))]
        bit //= 2
    while bit:
        found += [((a ^ bit, u), (b ^ bit, v)) for (a, u), (b, v) in found]
        bit //= 2
    return found


def crossed(value, entry):
    n_row, n_col = lax.axis_size("row"), lax.axis_size("col")
    pairs = []
    for r in range(n_row):
        q, u = entry[r % 2]
        pairs += [(r * n_col + c, (r ^ (2 * q)) * n_col + (c ^ u)) for c in range(n_col)]
    return lax.ppermute(value, BOTH, pairs)


def spread(found, near):
    while len(found) < len(near):
        found = found + [crossed(a, near[len(found)]) for a in found]
    return found


def swapped(value, q, u):
    n_row, n_col = lax.axis_size("row"), lax.axis_size("col")
    pairs = [(r * n_col + c, (r ^ q) * n_col + (c ^ u)) for r in range(n_row) for c in range(n_col)]
    return lax.ppermute(value, BOTH, pairs)


def per_device(start_block, matrix_tiles, tile_columns, history):
    n_row, n_col = lax.axis_size("row"), lax.axis_size("col")
    _, groups, _, slots, order, _ = matrix_tiles.shape
    n_vectors = start_block.shape[1]
    stored = history.shape[1]
    rows = groups * slots * order
    n_block = n_row // 2
    lanes = 2 if n_col % 2 == 0 else 1
    width = n_vectors // (n_block * lanes)
    members = n_col // lanes
    few = members <= 4
    near = neighbours(n_block, lanes)
    count = len(near)
    early = count - count // 4

    def over_members(value):
        return [value] + [swapped(value, 0, k * lanes) for k in range(1, members)]

    def mate(value):
        return swapped(value, 1, 0)

    plane = lanes == 2 and n_block > 1
    tiles = [matrix_tiles.reshape(rows, order)]
    if plane:
        tiles += lax.optimization_barrier([crossed(tiles[0], entry) for entry in near[1:3]])
        tiles.append(crossed(tiles[1], near[2]))
    tiles = spread(tiles, near)
    tall = -(-width // PAD) * PAD + PAD
    parts = call(
        functools.partial(prepare, lanes, width),
        jax.ShapeDtypeStruct((n_block, n_col, tall, order), BF16),
        (tile_columns.reshape(groups, slots).T, start_block),
    )
    cores = [
        [(2 * r + core) * n_col + c for r in range(n_block) for c in range(n_col)] for core in range(2)
    ]
    parts = lax.all_to_all(
        parts.reshape(n_block * n_col, tall, order), BOTH, 0, 0, axis_index_groups=cores
    ).reshape(n_block, n_col, tall, order)
    core = lax.axis_index("row") & 1
    half = stored // 2
    low, high = history[:, :half], history[:, half:]
    ours = jnp.where(core == 0, low, high)
    theirs = mate(jnp.where(core == 0, high, low))
    history = jnp.where(core == 0, jnp.stack([ours, theirs]), jnp.stack([theirs, ours]))
    own = [history]
    if plane:
        history, tiles[2] = lax.optimization_barrier((history, tiles[2]))
        own += [crossed(history, entry) for entry in near[1:3]]

    piece = (lanes, n_block, width, order)
    sums = ((lanes, groups, width, order), F32)
    before, columns, start = call(
        functools.partial(first, near, early, lanes, slots),
        [
            jax.ShapeDtypeStruct(sums[0], F32),
            jax.ShapeDtypeStruct((count, order, LINES), jnp.int32),
            jax.ShapeDtypeStruct(piece, BF16),
        ],
        (parts, *tiles[:early]),
    )
    keep, give = call(
        functools.partial(rest, near, early, slots),
        [jax.ShapeDtypeStruct(piece, F32)] * 2,
        (columns, parts, before, *tiles[early:]),
        [sums],
    )
    if plane:
        own.append(crossed(own[1], near[2]))
    own = spread(own, near)
    mine = (keep + mate(give)).astype(BF16)
    if few:
        vectors = over_members(mine)
    else:
        alike = [list(range(u, n_col, lanes)) for u in range(lanes)]
        vectors = [
            lax.all_to_all(
                jnp.broadcast_to(mine, (members,) + piece), "col", 0, 0, axis_index_groups=alike
            )
        ]
    ours = call(
        functools.partial(second, near, slots, len(vectors)),
        jax.ShapeDtypeStruct(sums[0], F32),
        (columns, start, *vectors, *tiles),
        [sums] + ([((members,) + piece, BF16)] if few else []),
    )
    filtered, coeffs = call(
        functools.partial(project, near),
        [jax.ShapeDtypeStruct(sums[0], F32), jax.ShapeDtypeStruct((width, half), F32)],
        (ours, mate(ours), *own),
    )
    if members == 4:
        zero, one, two, three = over_members(coeffs)
        coeffs = (zero + one) + (two + three)
    else:
        step = lanes
        while step < n_col:
            coeffs = coeffs + swapped(coeffs, 0, step)
            step *= 2
    slab = jax.ShapeDtypeStruct((width, stored + order), F32)
    copies = 1
    while nbytes(slab) > 2 * n_row * n_col * copies * n_vectors * 4:
        copies *= 2
    keep, give = call(
        functools.partial(correct, near),
        [jax.ShapeDtypeStruct(piece, F32)] * 2,
        (coeffs, *own),
    )
    *slabs, squares = call(
        functools.partial(clean, near),
        [slab] * count + [jax.ShapeDtypeStruct((n_row * n_col, copies, n_vectors), F32)],
        (coeffs, mate(coeffs), filtered, keep, mate(give)),
    )
    slabs = [slabs[0]] + [crossed(a, entry) for a, entry in zip(slabs[1:], near[1:])]
    squares = lax.all_to_all(squares, BOTH, 0, 0)
    return call(
        functools.partial(finish, near, lanes, order * n_row * n_col),
        (
            jax.ShapeDtypeStruct((order, n_vectors), F32),
            jax.ShapeDtypeStruct((stored, n_vectors), F32),
        ),
        (squares, *slabs[::-1]),
        [((n_vectors, stored + order), F32)],
    )


def solution(mesh):
    in_specs = (
        P(("row", "col"), None),
        P("row", None, "col", None, None, None),
        P("row", None, "col", None),
        P(("row", "col"), None),
    )
    out_specs = (P(("row", "col"), None), P())
    return jax.shard_map(
        per_device, mesh=mesh, in_specs=in_specs, out_specs=out_specs, check_vma=False
    )
```

```python
import functools

import jax
import jax.numpy as jnp
from jax import lax
from jax.experimental import pallas as pl
from jax.experimental.pallas import tpu as pltpu
from jax.sharding import PartitionSpec as P

F32 = jnp.float32
BF16 = jnp.bfloat16
PAD = 16
LINES = 8
VMEM = pl.BlockSpec(memory_space=pltpu.VMEM)
BOTH = ("row", "col")


def nbytes(tree):
    return sum(a.size * a.dtype.itemsize for a in jax.tree.leaves(tree))


def call(kernel, out, args, scratch=()):
    held = [jax.ShapeDtypeStruct(shape, kind) for shape, kind in scratch]
    room = 2 * (nbytes(args) + nbytes(out) + nbytes(held)) + 8 * 2**20
    return pl.pallas_call(
        kernel,
        out_shape=out,
        in_specs=[VMEM] * len(args),
        out_specs=jax.tree.map(lambda _: VMEM, out),
        scratch_shapes=[pltpu.VMEM(shape, kind) for shape, kind in scratch],
        compiler_params=pltpu.CompilerParams(vmem_limit_bytes=min(room, 56 * 2**20)),
    )(*args)


def position(lanes):
    row, col = lax.axis_index("row"), lax.axis_index("col")
    return row >> 1, row & 1, col >> (lanes - 1), col & (lanes - 1)


def place(entry, core):
    (even_q, even_u), (odd_q, odd_u) = entry
    return jnp.where(core == 0, even_q, odd_q), jnp.where(core == 0, even_u, odd_u)


def nt(a, b):
    return lax.dot_general(a, b, (((1,), (1,)), ((), ())), preferred_element_type=F32)


def pieces(value):
    high = value.astype(BF16)
    rest = value - high.astype(F32)
    middle = rest.astype(BF16)
    low = (rest - middle.astype(F32)).astype(BF16)
    return jnp.concatenate([high, middle, low], axis=0)


def joined(stacked):
    third = stacked.shape[0] // 3
    return (stacked[2 * third :] + stacked[third : 2 * third]) + stacked[:third]


def each(count, body):
    if count <= 4:
        for i in range(count):
            body(i)
    else:
        pl.loop(0, count)(body)


def prepare(lanes, width, columns_ref, start_ref, parts_ref):
    n_block, n_col, rows, order = parts_ref.shape
    slots, groups = columns_ref.shape
    lane = lax.broadcasted_iota(jnp.int32, (PAD, order), 1)
    numbers = jnp.zeros(lane.shape, jnp.int32)
    for p in range(groups):
        for s in range(slots):
            numbers = jnp.where(lane == p * slots + s, columns_ref[s, p], numbers)
    numbers = numbers.astype(F32).astype(BF16)
    turned = start_ref[...].astype(F32).T
    for r in range(n_block):
        for u in range(lanes):
            first_row = (r * lanes + u) * width
            part = turned[first_row : first_row + width].astype(BF16)
            for c in range(u, n_col, lanes):
                parts_ref[r, c, :width] = part
                parts_ref[r, c, rows - PAD :] = numbers


def multiply(near, lanes, slots, columns_ref, segment, tiles, sums_ref):
    groups, order = sums_ref.shape[1], sums_ref.shape[3]
    block, core, _, _ = position(lanes)
    for i, tile_ref in tiles:
        q, u = place(near[i], core)

        def row(p):
            picked, kept = [], []
            for s in range(slots):
                start = (p * slots + s) * order
                if not isinstance(start, int):
                    start = pl.multiple_of(start, order)
                picked.append(segment(block ^ q, columns_ref[i, p * slots + s, 0]))
                kept.append(tile_ref[pl.ds(start, order), :])
            sums_ref[u, p] += nt(jnp.concatenate(picked, axis=1), jnp.concatenate(kept, axis=1))

        each(groups, row)


def first(near, early, lanes, slots, parts_ref, *refs):
    tiles, (sums_ref, columns_ref, start_ref) = refs[:early], refs[early:]
    _, groups, width, order = sums_ref.shape
    block, core, me_z, me_lane = position(lanes)
    rows = parts_ref.shape[2]
    for i, entry in enumerate(near):
        q, u = place(entry, core)
        numbers = parts_ref[block ^ q, me_z * lanes + (me_lane ^ u), rows - PAD :]
        columns_ref[i] = numbers.astype(F32)[:LINES].T.astype(jnp.int32)
    for u in range(lanes):
        for r in range(parts_ref.shape[0]):
            start_ref[u, r] = parts_ref[r, me_z * lanes + (me_lane ^ u), :width]
    sums_ref[...] = jnp.zeros_like(sums_ref)
    multiply(
        near, lanes, slots, columns_ref, lambda b, c: parts_ref[b, c, :width],
        list(enumerate(tiles)), sums_ref,
    )


def rest(near, early, slots, columns_ref, parts_ref, before_ref, *refs):
    tiles, (keep_ref, give_ref, sums_ref) = refs[: len(near) - early], refs[len(near) - early :]
    lanes, n_block, width, _ = keep_ref.shape
    _, core, _, _ = position(lanes)
    sums_ref[...] = before_ref[...]
    multiply(
        near, lanes, slots, columns_ref, lambda b, c: parts_ref[b, c, :width],
        list(enumerate(tiles, early)), sums_ref,
    )
    for u in range(lanes):
        for r in range(n_block):
            keep_ref[u, r] = sums_ref[u, 2 * r + core]
            give_ref[u, r] = sums_ref[u, 2 * r + (1 - core)]


def second(near, slots, n_vectors, columns_ref, start_ref, *refs):
    count = len(near)
    vectors, tiles, refs = refs[:n_vectors], refs[n_vectors : n_vectors + count], refs[n_vectors + count :]
    out_ref, sums_ref = refs[:2]
    lanes, n_block, _, _ = start_ref.shape
    _, core, me_z, me_lane = position(lanes)
    if n_vectors > 1:
        all_ref = refs[2]
        for k in range(n_vectors):
            all_ref[me_z ^ k] = vectors[k][...]
    else:
        all_ref = vectors[0]

    def segment(b, c):
        return all_ref[c >> (lanes - 1), (c & (lanes - 1)) ^ me_lane, b]

    sums_ref[...] = jnp.zeros_like(sums_ref)
    multiply(near, lanes, slots, columns_ref, segment, list(enumerate(tiles)), sums_ref)
    for u in range(lanes):
        for r in range(n_block):
            out_ref[u, 2 * r + core] = 2.0 * sums_ref[u, 2 * r + core] - start_ref[u, r].astype(F32)
            out_ref[u, 2 * r + (1 - core)] = 2.0 * sums_ref[u, 2 * r + (1 - core)]


def project(near, ours_ref, theirs_ref, *refs):
    history, (filtered_ref, coeffs_ref) = refs[: len(near)], refs[len(near) :]
    lanes = ours_ref.shape[0]
    block, core, _, _ = position(lanes)
    filtered_ref[...] = ours_ref[...] + theirs_ref[...]
    total = None
    for i, entry in enumerate(near):
        q, u = place(entry, core)
        for side in range(2):
            split = pieces(filtered_ref[u, 2 * (block ^ q) + side])
            term = joined(jnp.dot(split, history[i][side], preferred_element_type=F32))
            total = term if total is None else total + term
    coeffs_ref[...] = total


def correct(near, coeffs_ref, *refs):
    history, (keep_ref, give_ref) = refs[: len(near)], refs[len(near) :]
    lanes = keep_ref.shape[0]
    block, core, _, _ = position(lanes)
    split = pieces(coeffs_ref[...])
    for i, entry in enumerate(near):
        q, u = place(entry, core)
        keep_ref[u, block ^ q] = joined(nt(split, history[i][core]))
        give_ref[u, block ^ q] = joined(nt(split, history[i][1 - core]))


def clean(near, mine_ref, mate_ref, filtered_ref, ours_ref, theirs_ref, *refs):
    count = len(near)
    outs, squares_ref = refs[:count], refs[count]
    lanes, _, width, order = ours_ref.shape
    block, core, _, me_lane = position(lanes)
    mine, mate = mine_ref[...], mate_ref[...]
    coeffs = jnp.concatenate(
        [jnp.where(core == 0, mine, mate), jnp.where(core == 0, mate, mine)], axis=1
    )
    stored = coeffs.shape[1]
    squares = jnp.zeros((width, order), F32)
    for i, entry in enumerate(near):
        q, u = place(entry, core)
        r = block ^ q
        cleaned = filtered_ref[u, 2 * r + core] - (ours_ref[u, r] + theirs_ref[u, r])
        squares = squares + cleaned * cleaned
        outs[i][:, :stored] = coeffs
        outs[i][:, stored:] = cleaned
    sums = jnp.sum(squares.T, axis=0, keepdims=True)
    n_vectors = squares_ref.shape[2]
    line = jnp.concatenate([sums] * (n_vectors // width), axis=1)
    lane = lax.broadcasted_iota(jnp.int32, line.shape, 1)
    begin = (block * lanes + me_lane) * width
    line = jnp.where((lane >= begin) & (lane < begin + width), line, 0.0)
    squares_ref[...] = jnp.broadcast_to(line[:, None, :], squares_ref.shape)


def finish(near, lanes, total_rows, squares_ref, *refs):
    slabs, (block_ref, out_ref, whole_ref) = refs[:-3], refs[-3:]
    width = slabs[0].shape[0]
    stored = out_ref.shape[0]
    block, core, _, me_lane = position(lanes)
    for slab, entry in zip(slabs, near[::-1]):
        q, u = place(entry, core)
        start = ((block ^ q) * lanes + (me_lane ^ u)) * width
        whole_ref[pl.ds(pl.multiple_of(start, width), width), :] = slab[...]
    sums = jnp.sum(squares_ref[...], axis=0)[:1]
    lengths = jnp.sqrt(sums / total_rows + 1e-05)
    out_ref[...] = whole_ref[:, :stored].T
    block_ref[...] = whole_ref[:, stored:].T / lengths


def neighbours(n_block, lanes):
    found = [((0, 0), (0, 0))]
    bit = n_block // 2
    if lanes == 2:
        found.append(((0, 1), (bit, 0)) if bit else ((0, 1), (0, 1)))
    if lanes == 2 and bit:
        found += [((bit, 0), (0, 1)), ((bit, 1), (bit, 1))]
        bit //= 2
    while bit:
        found += [((a ^ bit, u), (b ^ bit, v)) for (a, u), (b, v) in found]
        bit //= 2
    return found


def crossed(value, entry):
    n_row, n_col = lax.axis_size("row"), lax.axis_size("col")
    pairs = []
    for r in range(n_row):
        q, u = entry[r % 2]
        pairs += [(r * n_col + c, (r ^ (2 * q)) * n_col + (c ^ u)) for c in range(n_col)]
    return lax.ppermute(value, BOTH, pairs)


def spread(found, near):
    while len(found) < len(near):
        found = found + [crossed(a, near[len(found)]) for a in found]
    return found


def swapped(value, q, u):
    n_row, n_col = lax.axis_size("row"), lax.axis_size("col")
    pairs = [(r * n_col + c, (r ^ q) * n_col + (c ^ u)) for r in range(n_row) for c in range(n_col)]
    return lax.ppermute(value, BOTH, pairs)


def per_device(start_block, matrix_tiles, tile_columns, history):
    n_row, n_col = lax.axis_size("row"), lax.axis_size("col")
    _, groups, _, slots, order, _ = matrix_tiles.shape
    n_vectors = start_block.shape[1]
    stored = history.shape[1]
    rows = groups * slots * order
    n_block = n_row // 2
    lanes = 2 if n_col % 2 == 0 else 1
    width = n_vectors // (n_block * lanes)
    members = n_col // lanes
    few = members <= 4
    near = neighbours(n_block, lanes)
    count = len(near)
    early = count - count // 4

    def over_members(value):
        return [value] + [swapped(value, 0, k * lanes) for k in range(1, members)]

    def mate(value):
        return swapped(value, 1, 0)

    plane = lanes == 2 and n_block > 1
    tiles = [matrix_tiles.reshape(rows, order)]
    if plane:
        tiles += lax.optimization_barrier([crossed(tiles[0], entry) for entry in near[1:3]])
        tiles.append(crossed(tiles[1], near[2]))
    tiles = spread(tiles, near)
    tall = -(-width // PAD) * PAD + PAD
    parts = call(
        functools.partial(prepare, lanes, width),
        jax.ShapeDtypeStruct((n_block, n_col, tall, order), BF16),
        (tile_columns.reshape(groups, slots).T, start_block),
    )
    cores = [
        [(2 * r + core) * n_col + c for r in range(n_block) for c in range(n_col)] for core in range(2)
    ]
    parts = lax.all_to_all(
        parts.reshape(n_block * n_col, tall, order), BOTH, 0, 0, axis_index_groups=cores
    ).reshape(n_block, n_col, tall, order)
    core = lax.axis_index("row") & 1
    half = stored // 2
    low, high = history[:, :half], history[:, half:]
    ours = jnp.where(core == 0, low, high)
    theirs = mate(jnp.where(core == 0, high, low))
    history = jnp.where(core == 0, jnp.stack([ours, theirs]), jnp.stack([theirs, ours]))
    own = [history]
    if plane:
        history, tiles[2] = lax.optimization_barrier((history, tiles[2]))
        own += [crossed(history, entry) for entry in near[1:3]]

    piece = (lanes, n_block, width, order)
    sums = ((lanes, groups, width, order), F32)
    before, columns, start = call(
        functools.partial(first, near, early, lanes, slots),
        [
            jax.ShapeDtypeStruct(sums[0], F32),
            jax.ShapeDtypeStruct((count, order, LINES), jnp.int32),
            jax.ShapeDtypeStruct(piece, BF16),
        ],
        (parts, *tiles[:early]),
    )
    keep, give = call(
        functools.partial(rest, near, early, slots),
        [jax.ShapeDtypeStruct(piece, F32)] * 2,
        (columns, parts, before, *tiles[early:]),
        [sums],
    )
    if plane:
        own.append(crossed(own[1], near[2]))
    own = spread(own, near)
    mine = (keep + mate(give)).astype(BF16)
    if few:
        vectors = over_members(mine)
    else:
        alike = [list(range(u, n_col, lanes)) for u in range(lanes)]
        vectors = [
            lax.all_to_all(
                jnp.broadcast_to(mine, (members,) + piece), "col", 0, 0, axis_index_groups=alike
            )
        ]
    ours = call(
        functools.partial(second, near, slots, len(vectors)),
        jax.ShapeDtypeStruct(sums[0], F32),
        (columns, start, *vectors, *tiles),
        [sums] + ([((members,) + piece, BF16)] if few else []),
    )
    filtered, coeffs = call(
        functools.partial(project, near),
        [jax.ShapeDtypeStruct(sums[0], F32), jax.ShapeDtypeStruct((width, half), F32)],
        (ours, mate(ours), *own),
    )
    if members == 4:
        zero, one, two, three = over_members(coeffs)
        coeffs = (zero + one) + (two + three)
    else:
        step = lanes
        while step < n_col:
            coeffs = coeffs + swapped(coeffs, 0, step)
            step *= 2
    slab = jax.ShapeDtypeStruct((width, stored + order), F32)
    copies = 1
    while nbytes(slab) > 2 * n_row * n_col * copies * n_vectors * 4:
        copies *= 2
    keep, give = call(
        functools.partial(correct, near),
        [jax.ShapeDtypeStruct(piece, F32)] * 2,
        (coeffs, *own),
    )
    *slabs, squares = call(
        functools.partial(clean, near),
        [slab] * count + [jax.ShapeDtypeStruct((n_row * n_col, copies, n_vectors), F32)],
        (coeffs, mate(coeffs), filtered, keep, mate(give)),
    )
    slabs = [slabs[0]] + [crossed(a, entry) for a, entry in zip(slabs[1:], near[1:])]
    squares = lax.all_to_all(squares, BOTH, 0, 0)
    return call(
        functools.partial(finish, near, lanes, order * n_row * n_col),
        (
            jax.ShapeDtypeStruct((order, n_vectors), F32),
            jax.ShapeDtypeStruct((stored, n_vectors), F32),
        ),
        (squares, *slabs[::-1]),
        [((n_vectors, stored + order), F32)],
    )


def solution(mesh):
    in_specs = (
        P(("row", "col"), None),
        P("row", None, "col", None, None, None),
        P("row", None, "col", None),
        P(("row", "col"), None),
    )
    out_specs = (P(("row", "col"), None), P())
    return jax.shard_map(
        per_device, mesh=mesh, in_specs=in_specs, out_specs=out_specs, check_vma=False
    )
```

```python
import functools

import jax
import jax.numpy as jnp
from jax import lax
from jax.experimental import pallas as pl
from jax.experimental.pallas import tpu as pltpu
from jax.sharding import PartitionSpec as P

F32 = jnp.float32
BF16 = jnp.bfloat16
PAD = 16
LINES = 8
VMEM = pl.BlockSpec(memory_space=pltpu.VMEM)
BOTH = ("row", "col")


def nbytes(tree):
    return sum(a.size * a.dtype.itemsize for a in jax.tree.leaves(tree))


def call(kernel, out, args, scratch=()):
    held = [jax.ShapeDtypeStruct(shape, kind) for shape, kind in scratch]
    room = 2 * (nbytes(args) + nbytes(out) + nbytes(held)) + 8 * 2**20
    return pl.pallas_call(
        kernel,
        out_shape=out,
        in_specs=[VMEM] * len(args),
        out_specs=jax.tree.map(lambda _: VMEM, out),
        scratch_shapes=[pltpu.VMEM(shape, kind) for shape, kind in scratch],
        compiler_params=pltpu.CompilerParams(vmem_limit_bytes=min(room, 56 * 2**20)),
    )(*args)


def position(lanes):
    row, col = lax.axis_index("row"), lax.axis_index("col")
    return row >> 1, row & 1, col >> (lanes - 1), col & (lanes - 1)


def place(entry, core):
    (even_q, even_u), (odd_q, odd_u) = entry
    return jnp.where(core == 0, even_q, odd_q), jnp.where(core == 0, even_u, odd_u)


def gray(k):
    return k ^ (k >> 1)


def nt(a, b):
    return lax.dot_general(a, b, (((1,), (1,)), ((), ())), preferred_element_type=F32)


def pieces(value):
    high = value.astype(BF16)
    rest = value - high.astype(F32)
    middle = rest.astype(BF16)
    low = (rest - middle.astype(F32)).astype(BF16)
    return jnp.concatenate([high, middle, low], axis=0)


def joined(stacked):
    third = stacked.shape[0] // 3
    return (stacked[2 * third :] + stacked[third : 2 * third]) + stacked[:third]


def each(count, body):
    if count <= 4:
        for i in range(count):
            body(i)
    else:
        pl.loop(0, count)(body)


def prepare(lanes, width, columns_ref, start_ref, parts_ref):
    n_block, n_col, rows, order = parts_ref.shape
    slots, groups = columns_ref.shape
    lane = lax.broadcasted_iota(jnp.int32, (PAD, order), 1)
    numbers = jnp.zeros(lane.shape, jnp.int32)
    for p in range(groups):
        for s in range(slots):
            numbers = jnp.where(lane == p * slots + s, columns_ref[s, p], numbers)
    numbers = numbers.astype(F32).astype(BF16)
    turned = start_ref[...].astype(F32).T
    for r in range(n_block):
        for u in range(lanes):
            first_row = (r * lanes + u) * width
            part = turned[first_row : first_row + width].astype(BF16)
            for c in range(u, n_col, lanes):
                parts_ref[r, c, :width] = part
                parts_ref[r, c, rows - PAD :] = numbers


def multiply(near, lanes, slots, columns_ref, segment, tiles, sums_ref):
    groups, order = sums_ref.shape[1], sums_ref.shape[3]
    block, core, _, _ = position(lanes)
    for i, tile_ref in tiles:
        q, u = place(near[i], core)

        def row(p):
            picked, kept = [], []
            for s in range(slots):
                start = (p * slots + s) * order
                if not isinstance(start, int):
                    start = pl.multiple_of(start, order)
                picked.append(segment(block ^ q, columns_ref[i, p * slots + s, 0]))
                kept.append(tile_ref[pl.ds(start, order), :])
            sums_ref[u, p] += nt(jnp.concatenate(picked, axis=1), jnp.concatenate(kept, axis=1))

        each(groups, row)


def first(near, early, lanes, slots, parts_ref, *refs):
    tiles, (sums_ref, columns_ref, start_ref) = refs[:early], refs[early:]
    _, groups, width, order = sums_ref.shape
    block, core, me_z, me_lane = position(lanes)
    rows = parts_ref.shape[2]
    for i, entry in enumerate(near):
        q, u = place(entry, core)
        numbers = parts_ref[block ^ q, me_z * lanes + (me_lane ^ u), rows - PAD :]
        columns_ref[i] = numbers.astype(F32)[:LINES].T.astype(jnp.int32)
    for u in range(lanes):
        for r in range(parts_ref.shape[0]):
            start_ref[u, r] = parts_ref[r, me_z * lanes + (me_lane ^ u), :width]
    sums_ref[...] = jnp.zeros_like(sums_ref)
    multiply(
        near, lanes, slots, columns_ref, lambda b, c: parts_ref[b, c, :width],
        list(enumerate(tiles)), sums_ref,
    )


def rest(near, early, slots, columns_ref, parts_ref, before_ref, *refs):
    tiles, (keep_ref, give_ref, sums_ref) = refs[: len(near) - early], refs[len(near) - early :]
    lanes, n_block, width, _ = keep_ref.shape
    _, core, _, _ = position(lanes)
    sums_ref[...] = before_ref[...]
    multiply(
        near, lanes, slots, columns_ref, lambda b, c: parts_ref[b, c, :width],
        list(enumerate(tiles, early)), sums_ref,
    )
    for u in range(lanes):
        for r in range(n_block):
            keep_ref[u, r] = sums_ref[u, 2 * r + core]
            give_ref[u, r] = sums_ref[u, 2 * r + (1 - core)]


def second(near, slots, n_vectors, columns_ref, start_ref, *refs):
    count = len(near)
    vectors, tiles, refs = refs[:n_vectors], refs[n_vectors : n_vectors + count], refs[n_vectors + count :]
    out_ref, sums_ref = refs[:2]
    lanes, n_block, _, _ = start_ref.shape
    _, core, me_z, me_lane = position(lanes)
    if n_vectors > 1:
        all_ref = refs[2]
        for k in range(n_vectors):
            all_ref[me_z ^ gray(k)] = vectors[k][...]
    else:
        all_ref = vectors[0]

    def segment(b, c):
        return all_ref[c >> (lanes - 1), (c & (lanes - 1)) ^ me_lane, b]

    sums_ref[...] = jnp.zeros_like(sums_ref)
    multiply(near, lanes, slots, columns_ref, segment, list(enumerate(tiles)), sums_ref)
    for u in range(lanes):
        for r in range(n_block):
            out_ref[u, 2 * r + core] = 2.0 * sums_ref[u, 2 * r + core] - start_ref[u, r].astype(F32)
            out_ref[u, 2 * r + (1 - core)] = 2.0 * sums_ref[u, 2 * r + (1 - core)]


def project(near, ours_ref, theirs_ref, *refs):
    history, (filtered_ref, coeffs_ref) = refs[: len(near)], refs[len(near) :]
    lanes = ours_ref.shape[0]
    block, core, _, _ = position(lanes)
    filtered_ref[...] = ours_ref[...] + theirs_ref[...]
    total = None
    for i, entry in enumerate(near):
        q, u = place(entry, core)
        for side in range(2):
            split = pieces(filtered_ref[u, 2 * (block ^ q) + side])
            term = joined(jnp.dot(split, history[i][side], preferred_element_type=F32))
            total = term if total is None else total + term
    coeffs_ref[...] = total


def correct(near, coeffs_ref, *refs):
    history, (keep_ref, give_ref) = refs[: len(near)], refs[len(near) :]
    lanes = keep_ref.shape[0]
    block, core, _, _ = position(lanes)
    split = pieces(coeffs_ref[...])
    for i, entry in enumerate(near):
        q, u = place(entry, core)
        keep_ref[u, block ^ q] = joined(nt(split, history[i][core]))
        give_ref[u, block ^ q] = joined(nt(split, history[i][1 - core]))


def clean(near, mine_ref, mate_ref, filtered_ref, ours_ref, theirs_ref, *refs):
    count = len(near)
    outs, squares_ref = refs[:count], refs[count]
    lanes, _, width, order = ours_ref.shape
    block, core, _, me_lane = position(lanes)
    mine, mate = mine_ref[...], mate_ref[...]
    coeffs = jnp.concatenate(
        [jnp.where(core == 0, mine, mate), jnp.where(core == 0, mate, mine)], axis=1
    )
    stored = coeffs.shape[1]
    squares = jnp.zeros((width, order), F32)
    for i, entry in enumerate(near):
        q, u = place(entry, core)
        r = block ^ q
        cleaned = filtered_ref[u, 2 * r + core] - (ours_ref[u, r] + theirs_ref[u, r])
        squares = squares + cleaned * cleaned
        outs[i][:, :stored] = coeffs
        outs[i][:, stored:] = cleaned
    sums = jnp.sum(squares.T, axis=0, keepdims=True)
    n_vectors = squares_ref.shape[2]
    line = jnp.concatenate([sums] * (n_vectors // width), axis=1)
    lane = lax.broadcasted_iota(jnp.int32, line.shape, 1)
    begin = (block * lanes + me_lane) * width
    line = jnp.where((lane >= begin) & (lane < begin + width), line, 0.0)
    squares_ref[...] = jnp.broadcast_to(line[:, None, :], squares_ref.shape)


def finish(near, lanes, total_rows, squares_ref, *refs):
    slabs, (block_ref, out_ref, whole_ref) = refs[:-3], refs[-3:]
    width = slabs[0].shape[0]
    stored = out_ref.shape[0]
    block, core, _, me_lane = position(lanes)
    for slab, entry in zip(slabs, near[::-1]):
        q, u = place(entry, core)
        start = ((block ^ q) * lanes + (me_lane ^ u)) * width
        whole_ref[pl.ds(pl.multiple_of(start, width), width), :] = slab[...]
    sums = jnp.sum(squares_ref[...], axis=0)[:1]
    lengths = jnp.sqrt(sums / total_rows + 1e-05)
    out_ref[...] = whole_ref[:, :stored].T
    block_ref[...] = whole_ref[:, stored:].T / lengths


def neighbours(n_block, lanes):
    found = [((0, 0), (0, 0))]
    bit = n_block // 2
    if lanes == 2:
        found.append(((0, 1), (bit, 0)) if bit else ((0, 1), (0, 1)))
    if lanes == 2 and bit:
        found += [((bit, 0), (0, 1)), ((bit, 1), (bit, 1))]
        bit //= 2
    while bit:
        found += [((a ^ bit, u), (b ^ bit, v)) for (a, u), (b, v) in found]
        bit //= 2
    return found


def crossed(value, entry):
    n_row, n_col = lax.axis_size("row"), lax.axis_size("col")
    pairs = []
    for r in range(n_row):
        q, u = entry[r % 2]
        pairs += [(r * n_col + c, (r ^ (2 * q)) * n_col + (c ^ u)) for c in range(n_col)]
    return lax.ppermute(value, BOTH, pairs)


def spread(found, near):
    while len(found) < len(near):
        found = found + [crossed(a, near[len(found)]) for a in found]
    return found


def swapped(value, q, u):
    n_row, n_col = lax.axis_size("row"), lax.axis_size("col")
    pairs = [(r * n_col + c, (r ^ q) * n_col + (c ^ u)) for r in range(n_row) for c in range(n_col)]
    return lax.ppermute(value, BOTH, pairs)


def per_device(start_block, matrix_tiles, tile_columns, history):
    n_row, n_col = lax.axis_size("row"), lax.axis_size("col")
    _, groups, _, slots, order, _ = matrix_tiles.shape
    n_vectors = start_block.shape[1]
    stored = history.shape[1]
    rows = groups * slots * order
    n_block = n_row // 2
    lanes = 2 if n_col % 2 == 0 else 1
    width = n_vectors // (n_block * lanes)
    members = n_col // lanes
    few = members <= 4
    near = neighbours(n_block, lanes)
    count = len(near)
    early = count - count // 4

    def over_members(value):
        return [value] + [swapped(value, 0, k * lanes) for k in range(1, members)]

    def mate(value):
        return swapped(value, 1, 0)

    plane = lanes == 2 and n_block > 1
    tiles = [matrix_tiles.reshape(rows, order)]
    if plane:
        tiles += lax.optimization_barrier([crossed(tiles[0], entry) for entry in near[1:3]])
        tiles.append(crossed(tiles[1], near[2]))
    tiles = spread(tiles, near)
    tall = -(-width // PAD) * PAD + PAD
    parts = call(
        functools.partial(prepare, lanes, width),
        jax.ShapeDtypeStruct((n_block, n_col, tall, order), BF16),
        (tile_columns.reshape(groups, slots).T, start_block),
    )
    cores = [
        [(2 * r + core) * n_col + c for r in range(n_block) for c in range(n_col)] for core in range(2)
    ]
    parts = lax.all_to_all(
        parts.reshape(n_block * n_col, tall, order), BOTH, 0, 0, axis_index_groups=cores
    ).reshape(n_block, n_col, tall, order)
    core = lax.axis_index("row") & 1
    half = stored // 2
    low, high = history[:, :half], history[:, half:]
    ours = jnp.where(core == 0, low, high)
    theirs = mate(jnp.where(core == 0, high, low))
    history = jnp.where(core == 0, jnp.stack([ours, theirs]), jnp.stack([theirs, ours]))
    own = [history]
    if plane:
        history, tiles[2] = lax.optimization_barrier((history, tiles[2]))
        own += [crossed(history, entry) for entry in near[1:3]]

    piece = (lanes, n_block, width, order)
    sums = ((lanes, groups, width, order), F32)
    before, columns, start = call(
        functools.partial(first, near, early, lanes, slots),
        [
            jax.ShapeDtypeStruct(sums[0], F32),
            jax.ShapeDtypeStruct((count, order, LINES), jnp.int32),
            jax.ShapeDtypeStruct(piece, BF16),
        ],
        (parts, *tiles[:early]),
    )
    keep, give = call(
        functools.partial(rest, near, early, slots),
        [jax.ShapeDtypeStruct(piece, F32)] * 2,
        (columns, parts, before, *tiles[early:]),
        [sums],
    )
    if plane:
        own.append(crossed(own[1], near[2]))
    own = spread(own, near)
    mine = (keep + mate(give)).astype(BF16)
    if few:
        vectors = [mine] + [swapped(mine, 0, gray(k) * lanes) for k in range(1, members)]
    else:
        alike = [list(range(u, n_col, lanes)) for u in range(lanes)]
        vectors = [
            lax.all_to_all(
                jnp.broadcast_to(mine, (members,) + piece), "col", 0, 0, axis_index_groups=alike
            )
        ]
    ours = call(
        functools.partial(second, near, slots, len(vectors)),
        jax.ShapeDtypeStruct(sums[0], F32),
        (columns, start, *vectors, *tiles),
        [sums] + ([((members,) + piece, BF16)] if few else []),
    )
    filtered, coeffs = call(
        functools.partial(project, near),
        [jax.ShapeDtypeStruct(sums[0], F32), jax.ShapeDtypeStruct((width, half), F32)],
        (ours, mate(ours), *own),
    )
    if members == 4:
        zero, one, two, three = over_members(coeffs)
        coeffs = (zero + one) + (three + two)
    else:
        step = lanes
        while step < n_col:
            coeffs = coeffs + swapped(coeffs, 0, step)
            step *= 2
    slab = jax.ShapeDtypeStruct((width, stored + order), F32)
    copies = 1
    while nbytes(slab) > 2 * n_row * n_col * copies * n_vectors * 4:
        copies *= 2
    keep, give = call(
        functools.partial(correct, near),
        [jax.ShapeDtypeStruct(piece, F32)] * 2,
        (coeffs, *own),
    )
    *slabs, squares = call(
        functools.partial(clean, near),
        [slab] * count + [jax.ShapeDtypeStruct((n_row * n_col, copies, n_vectors), F32)],
        (coeffs, mate(coeffs), filtered, keep, mate(give)),
    )
    slabs = [slabs[0]] + [crossed(a, entry) for a, entry in zip(slabs[1:], near[1:])]
    squares = lax.all_to_all(squares, BOTH, 0, 0)
    return call(
        functools.partial(finish, near, lanes, order * n_row * n_col),
        (
            jax.ShapeDtypeStruct((order, n_vectors), F32),
            jax.ShapeDtypeStruct((stored, n_vectors), F32),
        ),
        (squares, *slabs[::-1]),
        [((n_vectors, stored + order), F32)],
    )


def solution(mesh):
    in_specs = (
        P(("row", "col"), None),
        P("row", None, "col", None, None, None),
        P("row", None, "col", None),
        P(("row", "col"), None),
    )
    out_specs = (P(("row", "col"), None), P())
    return jax.shard_map(
        per_device, mesh=mesh, in_specs=in_specs, out_specs=out_specs, check_vma=False
    )
```

```python
import functools

import jax
import jax.numpy as jnp
from jax import lax
from jax.experimental import pallas as pl
from jax.experimental.pallas import tpu as pltpu
from jax.sharding import PartitionSpec as P

F32 = jnp.float32
BF16 = jnp.bfloat16
PAD = 16
LINES = 8
VMEM = pl.BlockSpec(memory_space=pltpu.VMEM)
BOTH = ("row", "col")


def nbytes(tree):
    return sum(a.size * a.dtype.itemsize for a in jax.tree.leaves(tree))


def call(kernel, out, args, scratch=()):
    held = [jax.ShapeDtypeStruct(shape, kind) for shape, kind in scratch]
    room = 2 * (nbytes(args) + nbytes(out) + nbytes(held)) + 8 * 2**20
    return pl.pallas_call(
        kernel,
        out_shape=out,
        in_specs=[VMEM] * len(args),
        out_specs=jax.tree.map(lambda _: VMEM, out),
        scratch_shapes=[pltpu.VMEM(shape, kind) for shape, kind in scratch],
        compiler_params=pltpu.CompilerParams(vmem_limit_bytes=min(room, 56 * 2**20)),
    )(*args)


def position(lanes):
    row, col = lax.axis_index("row"), lax.axis_index("col")
    return row >> 1, row & 1, col >> (lanes - 1), col & (lanes - 1)


def place(entry, core):
    (even_q, even_u), (odd_q, odd_u) = entry
    return jnp.where(core == 0, even_q, odd_q), jnp.where(core == 0, even_u, odd_u)


def nt(a, b):
    return lax.dot_general(a, b, (((1,), (1,)), ((), ())), preferred_element_type=F32)


def pieces(value):
    high = value.astype(BF16)
    rest = value - high.astype(F32)
    middle = rest.astype(BF16)
    low = (rest - middle.astype(F32)).astype(BF16)
    return jnp.concatenate([high, middle, low], axis=0)


def joined(stacked):
    third = stacked.shape[0] // 3
    return (stacked[2 * third :] + stacked[third : 2 * third]) + stacked[:third]


def each(count, body):
    if count <= 4:
        for i in range(count):
            body(i)
    else:
        pl.loop(0, count)(body)


def prepare(lanes, width, columns_ref, start_ref, parts_ref):
    n_block, n_col, rows, order = parts_ref.shape
    slots, groups = columns_ref.shape
    lane = lax.broadcasted_iota(jnp.int32, (PAD, order), 1)
    numbers = jnp.zeros(lane.shape, jnp.int32)
    for p in range(groups):
        for s in range(slots):
            numbers = jnp.where(lane == p * slots + s, columns_ref[s, p], numbers)
    numbers = numbers.astype(F32).astype(BF16)
    turned = start_ref[...].astype(F32).T
    for r in range(n_block):
        for u in range(lanes):
            first_row = (r * lanes + u) * width
            part = turned[first_row : first_row + width].astype(BF16)
            for c in range(u, n_col, lanes):
                parts_ref[r, c, :width] = part
                parts_ref[r, c, rows - PAD :] = numbers


def multiply(near, lanes, slots, columns_ref, segment, tiles, sums_ref):
    groups, order = sums_ref.shape[1], sums_ref.shape[3]
    block, core, _, _ = position(lanes)
    for i, tile_ref in tiles:
        q, u = place(near[i], core)

        def row(p):
            picked, kept = [], []
            for s in range(slots):
                start = (p * slots + s) * order
                if not isinstance(start, int):
                    start = pl.multiple_of(start, order)
                picked.append(segment(block ^ q, columns_ref[i, p * slots + s, 0]))
                kept.append(tile_ref[pl.ds(start, order), :])
            sums_ref[u, p] += nt(jnp.concatenate(picked, axis=1), jnp.concatenate(kept, axis=1))

        each(groups, row)


def first(near, early, lanes, slots, parts_ref, *refs):
    tiles, (sums_ref, columns_ref, start_ref) = refs[:early], refs[early:]
    _, groups, width, order = sums_ref.shape
    block, core, me_z, me_lane = position(lanes)
    rows = parts_ref.shape[2]
    for i, entry in enumerate(near):
        q, u = place(entry, core)
        numbers = parts_ref[block ^ q, me_z * lanes + (me_lane ^ u), rows - PAD :]
        columns_ref[i] = numbers.astype(F32)[:LINES].T.astype(jnp.int32)
    for u in range(lanes):
        for r in range(parts_ref.shape[0]):
            start_ref[u, r] = parts_ref[r, me_z * lanes + (me_lane ^ u), :width]
    sums_ref[...] = jnp.zeros_like(sums_ref)
    multiply(
        near, lanes, slots, columns_ref, lambda b, c: parts_ref[b, c, :width],
        list(enumerate(tiles)), sums_ref,
    )


def rest(near, early, slots, columns_ref, parts_ref, before_ref, *refs):
    tiles, (keep_ref, give_ref, sums_ref) = refs[: len(near) - early], refs[len(near) - early :]
    lanes, n_block, width, _ = keep_ref.shape
    _, core, _, _ = position(lanes)
    sums_ref[...] = before_ref[...]
    multiply(
        near, lanes, slots, columns_ref, lambda b, c: parts_ref[b, c, :width],
        list(enumerate(tiles, early)), sums_ref,
    )
    for u in range(lanes):
        for r in range(n_block):
            keep_ref[u, r] = sums_ref[u, 2 * r + core]
            give_ref[u, r] = sums_ref[u, 2 * r + (1 - core)]


def second(near, slots, n_vectors, columns_ref, start_ref, *refs):
    count = len(near)
    vectors, tiles, refs = refs[:n_vectors], refs[n_vectors : n_vectors + count], refs[n_vectors + count :]
    out_ref, sums_ref = refs[:2]
    lanes, n_block, _, _ = start_ref.shape
    _, core, me_z, me_lane = position(lanes)
    if n_vectors > 1:
        all_ref = refs[2]
        for k in range(n_vectors):
            all_ref[me_z ^ k] = vectors[k][...]
    else:
        all_ref = vectors[0]

    def segment(b, c):
        return all_ref[c >> (lanes - 1), (c & (lanes - 1)) ^ me_lane, b]

    sums_ref[...] = jnp.zeros_like(sums_ref)
    multiply(near, lanes, slots, columns_ref, segment, list(enumerate(tiles)), sums_ref)
    for u in range(lanes):
        for r in range(n_block):
            out_ref[u, 2 * r + core] = 2.0 * sums_ref[u, 2 * r + core] - start_ref[u, r].astype(F32)
            out_ref[u, 2 * r + (1 - core)] = 2.0 * sums_ref[u, 2 * r + (1 - core)]


def project(near, ours_ref, theirs_ref, *refs):
    history, (filtered_ref, coeffs_ref) = refs[: len(near)], refs[len(near) :]
    lanes = ours_ref.shape[0]
    block, core, _, _ = position(lanes)
    filtered_ref[...] = ours_ref[...] + theirs_ref[...]
    total = None
    for i, entry in enumerate(near):
        q, u = place(entry, core)
        for side in range(2):
            split = pieces(filtered_ref[u, 2 * (block ^ q) + side])
            term = joined(jnp.dot(split, history[i][side], preferred_element_type=F32))
            total = term if total is None else total + term
    coeffs_ref[...] = total


def correct(near, coeffs_ref, *refs):
    history, (keep_ref, give_ref) = refs[: len(near)], refs[len(near) :]
    lanes = keep_ref.shape[0]
    block, core, _, _ = position(lanes)
    split = pieces(coeffs_ref[...])
    for i, entry in enumerate(near):
        q, u = place(entry, core)
        keep_ref[u, block ^ q] = joined(nt(split, history[i][core]))
        give_ref[u, block ^ q] = joined(nt(split, history[i][1 - core]))


def clean(near, mine_ref, mate_ref, filtered_ref, ours_ref, theirs_ref, *refs):
    count = len(near)
    outs, squares_ref = refs[:count], refs[count]
    lanes, _, width, order = ours_ref.shape
    block, core, _, me_lane = position(lanes)
    mine, mate = mine_ref[...], mate_ref[...]
    coeffs = jnp.concatenate(
        [jnp.where(core == 0, mine, mate), jnp.where(core == 0, mate, mine)], axis=1
    )
    stored = coeffs.shape[1]
    squares = jnp.zeros((width, order), F32)
    for i, entry in enumerate(near):
        q, u = place(entry, core)
        r = block ^ q
        cleaned = filtered_ref[u, 2 * r + core] - (ours_ref[u, r] + theirs_ref[u, r])
        squares = squares + cleaned * cleaned
        outs[i][:, :stored] = coeffs
        outs[i][:, stored:] = cleaned
    sums = jnp.sum(squares.T, axis=0, keepdims=True)
    n_vectors = squares_ref.shape[2]
    line = jnp.concatenate([sums] * (n_vectors // width), axis=1)
    lane = lax.broadcasted_iota(jnp.int32, line.shape, 1)
    begin = (block * lanes + me_lane) * width
    line = jnp.where((lane >= begin) & (lane < begin + width), line, 0.0)
    squares_ref[...] = jnp.broadcast_to(line[:, None, :], squares_ref.shape)


def finish(near, lanes, total_rows, squares_ref, *refs):
    slabs, (block_ref, out_ref, whole_ref) = refs[:-3], refs[-3:]
    width = slabs[0].shape[0]
    stored = out_ref.shape[0]
    block, core, _, me_lane = position(lanes)
    for slab, entry in zip(slabs, near[::-1]):
        q, u = place(entry, core)
        start = ((block ^ q) * lanes + (me_lane ^ u)) * width
        whole_ref[pl.ds(pl.multiple_of(start, width), width), :] = slab[...]
    sums = jnp.sum(squares_ref[...], axis=0)[:1]
    lengths = jnp.sqrt(sums / total_rows + 1e-05)
    out_ref[...] = whole_ref[:, :stored].T
    block_ref[...] = whole_ref[:, stored:].T / lengths


def neighbours(n_block, lanes):
    found = [((0, 0), (0, 0))]
    bit = n_block // 2
    if lanes == 2:
        found.append(((0, 1), (bit, 0)) if bit else ((0, 1), (0, 1)))
    if lanes == 2 and bit:
        found += [((bit, 0), (0, 1)), ((bit, 1), (bit, 1))]
        bit //= 2
    while bit:
        found += [((a ^ bit, u), (b ^ bit, v)) for (a, u), (b, v) in found]
        bit //= 2
    return found


def crossed(value, entry):
    n_row, n_col = lax.axis_size("row"), lax.axis_size("col")
    pairs = []
    for r in range(n_row):
        q, u = entry[r % 2]
        pairs += [(r * n_col + c, (r ^ (2 * q)) * n_col + (c ^ u)) for c in range(n_col)]
    return lax.ppermute(value, BOTH, pairs)


def spread(found, near):
    while len(found) < len(near):
        found = found + [crossed(a, near[len(found)]) for a in found]
    return found


def swapped(value, q, u):
    n_row, n_col = lax.axis_size("row"), lax.axis_size("col")
    pairs = [(r * n_col + c, (r ^ q) * n_col + (c ^ u)) for r in range(n_row) for c in range(n_col)]
    return lax.ppermute(value, BOTH, pairs)


def per_device(start_block, matrix_tiles, tile_columns, history):
    n_row, n_col = lax.axis_size("row"), lax.axis_size("col")
    _, groups, _, slots, order, _ = matrix_tiles.shape
    n_vectors = start_block.shape[1]
    stored = history.shape[1]
    rows = groups * slots * order
    n_block = n_row // 2
    lanes = 2 if n_col % 2 == 0 else 1
    width = n_vectors // (n_block * lanes)
    members = n_col // lanes
    few = members <= 4
    near = neighbours(n_block, lanes)
    count = len(near)
    early = count - count // 4

    def over_members(value):
        return [value] + [swapped(value, 0, k * lanes) for k in range(1, members)]

    def mate(value):
        return swapped(value, 1, 0)

    plane = lanes == 2 and n_block > 1
    tiles = [matrix_tiles.reshape(rows, order)]
    if plane:
        tiles += lax.optimization_barrier([crossed(tiles[0], entry) for entry in near[1:3]])
        tiles.append(crossed(tiles[1], near[2]))
    tiles = spread(tiles, near)
    tall = -(-width // PAD) * PAD + PAD
    parts = call(
        functools.partial(prepare, lanes, width),
        jax.ShapeDtypeStruct((n_block, n_col, tall, order), BF16),
        (tile_columns.reshape(groups, slots).T, start_block),
    )
    cores = [
        [(2 * r + core) * n_col + c for r in range(n_block) for c in range(n_col)] for core in range(2)
    ]
    parts = lax.all_to_all(
        parts.reshape(n_block * n_col, tall, order), BOTH, 0, 0, axis_index_groups=cores
    ).reshape(n_block, n_col, tall, order)
    core = lax.axis_index("row") & 1
    half = stored // 2
    low, high = history[:, :half], history[:, half:]
    ours = jnp.where(core == 0, low, high)
    theirs = mate(jnp.where(core == 0, high, low))
    history = jnp.where(core == 0, jnp.stack([ours, theirs]), jnp.stack([theirs, ours]))
    own = [history]
    if plane:
        own += [crossed(history, entry) for entry in near[1:3]]

    piece = (lanes, n_block, width, order)
    sums = ((lanes, groups, width, order), F32)
    before, columns, start = call(
        functools.partial(first, near, early, lanes, slots),
        [
            jax.ShapeDtypeStruct(sums[0], F32),
            jax.ShapeDtypeStruct((count, order, LINES), jnp.int32),
            jax.ShapeDtypeStruct(piece, BF16),
        ],
        (parts, *tiles[:early]),
    )
    keep, give = call(
        functools.partial(rest, near, early, slots),
        [jax.ShapeDtypeStruct(piece, F32)] * 2,
        (columns, parts, before, *tiles[early:]),
        [sums],
    )
    if plane:
        own.append(crossed(own[1], near[2]))
    own = spread(own, near)
    mine = (keep + mate(give)).astype(BF16)
    if few:
        vectors = over_members(mine)
    else:
        alike = [list(range(u, n_col, lanes)) for u in range(lanes)]
        vectors = [
            lax.all_to_all(
                jnp.broadcast_to(mine, (members,) + piece), "col", 0, 0, axis_index_groups=alike
            )
        ]
    ours = call(
        functools.partial(second, near, slots, len(vectors)),
        jax.ShapeDtypeStruct(sums[0], F32),
        (columns, start, *vectors, *tiles),
        [sums] + ([((members,) + piece, BF16)] if few else []),
    )
    filtered, coeffs = call(
        functools.partial(project, near),
        [jax.ShapeDtypeStruct(sums[0], F32), jax.ShapeDtypeStruct((width, half), F32)],
        (ours, mate(ours), *own),
    )
    if members == 4:
        zero, one, two, three = over_members(coeffs)
        coeffs = (zero + one) + (two + three)
    else:
        step = lanes
        while step < n_col:
            coeffs = coeffs + swapped(coeffs, 0, step)
            step *= 2
    slab = jax.ShapeDtypeStruct((width, stored + order), F32)
    copies = 1
    while nbytes(slab) > 2 * n_row * n_col * copies * n_vectors * 4:
        copies *= 2
    keep, give = call(
        functools.partial(correct, near),
        [jax.ShapeDtypeStruct(piece, F32)] * 2,
        (coeffs, *own),
    )
    *slabs, squares = call(
        functools.partial(clean, near),
        [slab] * count + [jax.ShapeDtypeStruct((n_row * n_col, copies, n_vectors), F32)],
        (coeffs, mate(coeffs), filtered, keep, mate(give)),
    )
    slabs = [slabs[0]] + [crossed(a, entry) for a, entry in zip(slabs[1:], near[1:])]
    squares = lax.all_to_all(squares, BOTH, 0, 0)
    return call(
        functools.partial(finish, near, lanes, order * n_row * n_col),
        (
            jax.ShapeDtypeStruct((order, n_vectors), F32),
            jax.ShapeDtypeStruct((stored, n_vectors), F32),
        ),
        (squares, *slabs[::-1]),
        [((n_vectors, stored + order), F32)],
    )


def solution(mesh):
    in_specs = (
        P(("row", "col"), None),
        P("row", None, "col", None, None, None),
        P("row", None, "col", None),
        P(("row", "col"), None),
    )
    out_specs = (P(("row", "col"), None), P())
    return jax.shard_map(
        per_device, mesh=mesh, in_specs=in_specs, out_specs=out_specs, check_vma=False
    )
```
